256 devices in a mesh: slab: 32 (over y, x, core), mem: 8 (over z).
Axes of the slice: x: 4, y: 4, z: 8, core: 2. Of those that a mesh axis runs over, the one named last changes fastest.
Arguments:
- prior_concentrations: float32 [64, 2048, 1024], P('mem', 'slab'), may hold values from -6 to 6
- kappa: float32 [2048, 1024], P('slab'), may hold values from 0.05 to 0.15
- east_face_transport: float32 [2048, 1024], P('slab'), may hold values from -0.08 to 0.08
- v_north: float32 [2048, 1024], P('slab'), may hold values from -0.08 to 0.08
- land: int32 [2048, 1024], P('slab'), may hold values 0 or 1
- obs_owner: int32 [4], replicated, may hold values from 0 to 31, as said below
- obs_offset: int32 [4, 256], replicated, may hold values from 0 to 65535, as said below
- obs_value: float32 [4, 256], replicated, may hold values from -6 to 6
- obs_var: float32 [4, 256], replicated, may hold values from 0.25 to 1
- obs_noise: float32 [4, 256, 64], replicated, may hold values from -6 to 6
Outputs:
- analysis: float32 [64, 2048, 1024], P(None, 'slab', 'mem')
The draws below stay inside these ranges and needn't reach their ends.
Inputs may be any that keep to these rules, and one draw needn't show every extreme that they name: Batch b observes only rows obs_owner[b] * 64 to obs_owner[b] * 64 + 63. The observed cell lies at row obs_owner * 64 + obs_offset // 1024 and column obs_offset % 1024; cells may repeat.
All inputs are finite; a program needn't handle non-finite values. No bound on the sum of `land` on one device may be relied on, other than what follows from the above.
Results may differ from the reference program's by a relative error of at most 0.00014.
Values sent between devices are 32-bit elements; how exact they have to be, the bound alone decides.
A program may use at most 128 MiB of HBM per device.

```python
import math
import jax
import jax.numpy as jnp
from jax import lax

R = 64
W = 1024
ENSEMBLE_SIZE = 64
STEPS = 2
BATCHES = 4
NOBS = 256
NR = 2048
LOC = 1024
N_SLAB = 32


def draw_obs_owner(key, part):
    key = jax.random.fold_in(key, 11)
    first_key, second_key = jax.random.split(key)
    chosen = jax.random.randint(first_key, (BATCHES,), 0, N_SLAB, dtype=jnp.int32)
    chosen = chosen.at[0].set(0).at[1].set(N_SLAB - 1)
    return chosen[jax.random.permutation(second_key, BATCHES)]


def draw_obs_offset(key, part):
    key = jax.random.fold_in(key, 23)
    offsets = jax.random.randint(key, (BATCHES, NOBS), 0, R * W, dtype=jnp.int32)
    return offsets.at[0, 0].set(0).at[0, 1].set(R * W - 1)


def with_ends(drawn, own_key, smallest, top_value):
    longest = drawn.shape.index(max(drawn.shape))
    spots = []
    for shift in (0, 1):
        where = [jax.random.randint(jax.random.fold_in(own_key, axis), (), 0, length) for axis, length in enumerate(drawn.shape)]
        where[longest] = (where[longest] + shift) % drawn.shape[longest]
        spots.append(tuple(where))
    return drawn.at[spots[0]].set(smallest).at[spots[1]].set(top_value)


def levels(rng, dims, pieces, low, top_value):
    def one(dim, shards_of):
        heights = jax.random.uniform(jax.random.fold_in(jax.random.fold_in(rng, 6), dim), (shards_of,), jnp.float32, low / len(pieces), top_value / len(pieces))
        return jnp.repeat(jnp.exp(heights), dims[dim] // shards_of).reshape((-1,) + (1,) * (len(dims) - dim - 1))

    level = one(*pieces[0])
    for cut in pieces[1:]:
        level = level * one(*cut)
    return level


def bell_draw(rng, extent, scale, reach, cuts=(), kind=jnp.bfloat16):
    result = jax.random.normal(rng, extent, jnp.float32) * scale
    if len(cuts) > 0:
        result = levels(rng, extent, cuts, -0.22, 0.18) * result
    return jnp.clip(result, min=-reach, max=reach).astype(kind)


def setup_inputs(seed: int = 0) -> dict:
    splits = jax.random.split(jax.random.key(seed), 11)
    return {
        "prior_concentrations": bell_draw(splits[0], (ENSEMBLE_SIZE, NR, W), 1.0, 6.0, ((0, 8), (1, 32)), jnp.float32),
        "kappa": jnp.clip(0.05 + 0.10000001 * jax.random.uniform(splits[1], (NR, W), jnp.float32) ** levels(splits[1], (NR, W), ((0, 32),), -0.2, 0.2), 0.05, 0.15),
        "east_face_transport": jnp.clip(jax.random.uniform(splits[2], (NR, W), jnp.float32, -0.08, 0.08) * levels(splits[2], (NR, W), ((0, 32),), -0.4, 0.0), -0.08, 0.08),
        "v_north": jnp.clip(jax.random.uniform(splits[3], (NR, W), jnp.float32, -0.08, 0.08) * levels(splits[3], (NR, W), ((0, 32),), -0.4, 0.0), -0.08, 0.08),
        "land": with_ends((jax.random.randint(splits[4], (NR, W), 0, 8) < 7).astype(jnp.int32), jax.random.fold_in(splits[4], 1), 0, 1),
        "obs_owner": draw_obs_owner(jax.random.fold_in(splits[10], 71), 0),
        "obs_offset": draw_obs_offset(jax.random.fold_in(splits[10], 71), 0),
        "obs_value": bell_draw(splits[7], (BATCHES, NOBS), 1.0, 6.0, (), jnp.float32),
        "obs_var": jnp.clip(jnp.exp(jax.random.uniform(splits[8], (BATCHES, NOBS), jnp.float32, math.log(0.25), math.log(1.0))), 0.25, 1.0),
        "obs_noise": bell_draw(splits[9], (BATCHES, NOBS, ENSEMBLE_SIZE), 1.0, 6.0, (), jnp.float32),
    }


PRECISE = lax.Precision.HIGHEST

def advance(concentration, static_fields):
    conduct = static_fields[0]
    wetness = static_fields[1]
    eastward = static_fields[2]
    northward = static_fields[3]
    diffuse_east = jnp.sqrt(conduct[:, :-1] * conduct[:, 1:])
    opened_east = wetness[:, :-1] * wetness[:, 1:]
    flow_east = eastward[:, :-1]
    eastward_flux_rows = diffuse_east * (concentration[..., :, :-1] - concentration[..., :, 1:]) + opened_east * (jnp.maximum(flow_east, 0.0) * concentration[..., :, :-1] + jnp.minimum(flow_east, 0.0) * concentration[..., :, 1:])
    diffuse_north = jnp.sqrt(conduct[:-1, :] * conduct[1:, :])
    opened_north = wetness[:-1, :] * wetness[1:, :]
    flow_north = northward[:-1, :]
    flux_north = diffuse_north * (concentration[..., :-1, :] - concentration[..., 1:, :]) + opened_north * (jnp.maximum(flow_north, 0.0) * concentration[..., :-1, :] + jnp.minimum(flow_north, 0.0) * concentration[..., 1:, :])
    change = eastward_flux_rows[..., 1:-1, 1:] - eastward_flux_rows[..., 1:-1, :-1] + flux_north[..., 1:, 1:-1] - flux_north[..., :-1, 1:-1]
    return wetness[1:-1, 1:-1] * (concentration[..., 1:-1, 1:-1] - change)

def solve_batch(priors, observed, variance, perturb):
    members = priors.shape[1]
    deviations = priors - lax.optimization_barrier(jnp.mean(priors, axis=1, keepdims=True))
    spread = jnp.dot(deviations, deviations.T, precision=PRECISE) / (members - 1) + jnp.diag(variance)
    misfit = observed[:, None] + jnp.sqrt(variance)[:, None] * perturb - priors
    return (deviations, jnp.linalg.solve(spread, misfit))

def apply_batch(states, deviations, weights, row_places, column_places, site_row, site_column, wet_flat, taper_rate):
    members = states.shape[0]
    anomalies = states - lax.optimization_barrier(jnp.mean(states, axis=0, keepdims=True))
    covariance = jnp.dot(deviations, anomalies, precision=PRECISE) / (members - 1)
    row_gap = (row_places[None, :] - site_row[:, None]).astype(jnp.float32)
    column_gap = (column_places[None, :] - site_column[:, None]).astype(jnp.float32)
    tapering = jnp.exp(-taper_rate * (row_gap * row_gap + column_gap * column_gap))
    return states + jnp.dot(weights.T, tapering * covariance, precision=PRECISE) * wet_flat[None, :]

def reference(prior_concentrations, kappa, east_face_transport, v_north, land, obs_owner, obs_offset, obs_value, obs_var, obs_noise):
    wetness = land.astype(jnp.float32)
    static_fields = jnp.stack([wetness * kappa, wetness, east_face_transport, v_north])
    static_padded = jnp.pad(static_fields, ((0, 0), (1, 1), (1, 1)))

    def predicted_concentration(realization_number):
        for step_number in range(STEPS):
            realization_number = advance(jnp.pad(realization_number, 1), static_padded)
        return realization_number
    concentration_maps = lax.map(predicted_concentration, prior_concentrations)
    cell_ids = (obs_owner[:, None] * (R * W) + obs_offset).astype(jnp.int32)
    site_rows = cell_ids // W
    site_columns = cell_ids % W
    taper_rate = 0.5 / (LOC * LOC)
    position = jnp.arange(R * W, dtype=jnp.int32)
    row_within = position // W
    column_within = position % W
    for batch_number in range(BATCHES):
        flattened = concentration_maps.reshape(ENSEMBLE_SIZE, NR * W)
        priors = jnp.take(flattened, cell_ids[batch_number], axis=1).T
        deviations, weights = solve_batch(priors, obs_value[batch_number], obs_var[batch_number], obs_noise[batch_number])

        def analysis_slab_update(slab_number, current):
            slab_number = jnp.asarray(slab_number).astype(jnp.int32)
            start = (slab_number * R).astype(jnp.int32)
            states = lax.dynamic_slice_in_dim(current, start, R, 1).reshape(ENSEMBLE_SIZE, R * W)
            wet_portion = lax.dynamic_slice_in_dim(wetness, start, R, 0).reshape(R * W)
            updated_members = apply_batch(states, deviations, weights, start + row_within, column_within, site_rows[batch_number], site_columns[batch_number], wet_portion, taper_rate)
            return lax.dynamic_update_slice_in_dim(current, updated_members.reshape(ENSEMBLE_SIZE, R, W), start, 1)
        concentration_maps = lax.fori_loop(0, N_SLAB, analysis_slab_update, concentration_maps)
    return concentration_maps
```

```python
import functools

import jax
import jax.numpy as jnp
from jax import lax
from jax.experimental import pallas as pl
from jax.experimental.pallas import tpu as pltpu
from jax.sharding import PartitionSpec as P

F32 = jnp.float32
BF16 = jnp.bfloat16
PRECISE = lax.Precision.HIGHEST
MESH = pl.DeviceIdType.MESH
LANES = 128
OWN = 8
BASE = 8


def contract(a, b, dims):
    return lax.dot_general(
        a, b, ((dims[:1], dims[1:]), ((), ())), precision=PRECISE, preferred_element_type=F32
    )


def quick(a, b):
    return jnp.dot(a, b, preferred_element_type=F32)


def split(x):
    high = x.astype(BF16)
    return high, (x - high.astype(F32)).astype(BF16)


def solve_spd(system):
    rows, lanes = system.shape
    at = lax.broadcasted_iota(jnp.int32, (8, lanes), 0)

    def block(_, parts):
        parts = list(parts)
        for k in range(8):
            head = parts[0]
            factors = [jnp.broadcast_to(p[:, k : k + 1], p.shape) for p in parts]
            pivot = head[k : k + 1, :] / factors[0][k : k + 1, :]
            parts = [p - f * pivot for p, f in zip(parts, factors)]
            parts[0] = jnp.where(at == k, pivot, parts[0])
        parts = [pltpu.roll(p, lanes - 8, 1) for p in parts]
        return tuple(parts[1:] + parts[:1])

    parts = tuple(system[8 * i : 8 * i + 8] for i in range(rows // 8))
    parts = lax.fori_loop(0, rows // 8, block, parts)
    return jnp.concatenate(parts, 0)[:, :rows]


def kernel(
    geometry,
    prior_ref,
    kappa_ref,
    east_ref,
    north_ref,
    land_ref,
    owner_ref,
    offset_ref,
    value_ref,
    var_ref,
    noise_ref,
    out_ref,
    padded,
    middle,
    forecast,
    states,
    stat_send,
    stat_recv,
    ext,
    coef,
    parts,
    column_of,
    line_of,
    sea,
    picked,
    reduce_buf,
    piece,
    gathered,
    sites,
    tapers,
    base_misfit,
    dcat,
    wcat,
    column_taper,
    row_site,
    wet_cols,
    site_cols,
    halo_send,
    halo_recv,
    reduce_send,
    reduce_recv,
    ring_send,
    ring_recv,
    share_send,
    share_recv,
    swap_send,
    swap_recv,
):
    n_slab, n_mem, n_piece, rb = geometry
    rows = kappa_ref.shape[0]
    width = kappa_ref.shape[1]
    members = OWN * n_mem
    batches, nobs = var_ref.shape
    total_obs = batches * nobs
    chunks = rows // rb
    extent = rows * n_slab // 2
    rate = 0.5 / (extent * extent)

    s = lax.axis_index("slab")
    z = lax.axis_index("mem")
    mine = lax.rem(s, n_piece)

    def slab_of(d):
        return lax.rem(s + d, n_slab)

    def mem_of(d):
        return lax.rem(z + d, n_mem)

    def piece_of(d):
        return s - mine + lax.rem(mine + d, n_piece)

    barrier = pltpu.get_barrier_semaphore()
    for d in range(1, n_slab):
        pl.semaphore_signal(barrier, inc=1, device_id=(slab_of(d), z), device_id_type=MESH)
    for d in range(1, n_mem):
        pl.semaphore_signal(barrier, inc=1, device_id=(s, mem_of(d)), device_id_type=MESH)

    def fill(r):
        tile = prior_ref[:, pl.ds(r, 8), :]
        padded[pl.ds(r + 2, 8)] = jnp.swapaxes(tile, 0, 1)

    wet = land_ref[...].astype(F32)
    ext[0, BASE : BASE + rows] = wet * kappa_ref[...]
    ext[1, BASE : BASE + rows] = wet
    ext[2, BASE : BASE + rows] = east_ref[...]
    ext[3, BASE : BASE + rows] = north_ref[...]
    for side, first in ((0, BASE), (1, BASE + rows - 2)):
        for field in range(4):
            stat_send[side, 2 * field : 2 * field + 2] = ext[field, first : first + 2]
    fill(0)
    fill(rows - 8)

    pl.semaphore_wait(barrier, n_slab - 1 + n_mem - 1)

    halo = []
    for side, (d, src, dst) in enumerate(
        ((n_slab - 1, 2, rows + 2), (1, rows, 0))
    ):
        target = (slab_of(d), z)
        halo.append(
            pltpu.make_async_remote_copy(
                src_ref=stat_send.at[side],
                dst_ref=stat_recv.at[side],
                send_sem=halo_send.at[2 * side],
                recv_sem=halo_recv.at[2 * side],
                device_id=target,
                device_id_type=MESH,
            )
        )
        halo.append(
            pltpu.make_async_remote_copy(
                src_ref=padded.at[pl.ds(src, 2)],
                dst_ref=padded.at[pl.ds(dst, 2)],
                send_sem=halo_send.at[2 * side + 1],
                recv_sem=halo_recv.at[2 * side + 1],
                device_id=target,
                device_id_type=MESH,
            )
        )
    for copy in halo:
        copy.start()

    def fill_rest(i, carry):
        fill(pl.multiple_of(8 * i, 8))
        return carry

    lax.fori_loop(1, rows // 8 - 1, fill_rest, 0)

    offsets = offset_ref[...]
    batch_at = lax.broadcasted_iota(jnp.int32, offsets.shape, 0)
    owner_rows = jnp.zeros(offsets.shape, jnp.int32)
    for b in range(batches):
        owner_rows = jnp.where(batch_at == b, owner_ref[b] * rows, owner_rows)
    site_row = (owner_rows + offsets // width).astype(F32)
    site_col = (offsets % width).astype(F32)
    sites[0:batches] = site_row
    sites[batches : 2 * batches] = site_col
    flipped = sites[...].T
    row0 = (s * rows).astype(F32)
    col0 = (z * LANES).astype(F32)
    columns = lax.broadcasted_iota(jnp.int32, (1, LANES), 1).astype(F32) + col0
    for b in range(batches):
        row_j = flipped[:, b : b + 1]
        col_j = flipped[:, batches + b : batches + b + 1]
        gap = col_j - columns
        column_taper[b] = jnp.exp(-rate * (gap * gap))
        row_site[b] = jnp.broadcast_to(row_j, (nobs, LANES)) - row0
        for later in range(b + 1, batches):
            g_row = row_j - sites[later : later + 1]
            g_col = col_j - sites[batches + later : batches + later + 1]
            tapers[b, :, nobs * later : nobs * (later + 1)] = jnp.exp(
                -rate * (g_row * g_row + g_col * g_col)
            )
        base_misfit[b] = (
            value_ref[b : b + 1] + jnp.sqrt(var_ref[b : b + 1]) * noise_ref[b].T
        )
    line_of[...] = jnp.where(owner_rows == s * rows, offsets // width, -1)
    for b in range(batches):
        column = (offsets % width)[b : b + 1]
        for first in range(0, width, nobs):
            at = lax.broadcasted_iota(jnp.int32, (nobs, nobs), 0) + first
            column_of[b, first : first + nobs] = (at == column).astype(F32).astype(BF16)
    sea[...] = wet.astype(BF16)
    wet_cols[...] = land_ref[:, pl.ds(pl.multiple_of(z * LANES, LANES), LANES)].astype(F32)

    for copy in halo:
        copy.wait()

    low_ok = (s > 0).astype(F32)
    high_ok = (s < n_slab - 1).astype(F32)
    for field in range(4):
        ext[field, BASE - 2 : BASE] = stat_recv[1, 2 * field : 2 * field + 2] * low_ok
        ext[field, BASE + rows : BASE + rows + 2] = (
            stat_recv[0, 2 * field : 2 * field + 2] * high_ok
        )

    tall = ext.shape[1]
    lane = lax.broadcasted_iota(jnp.int32, (1, width), 1)
    not_last = (lane < width - 1).astype(F32)
    not_first = (lane > 0).astype(F32)

    def coefficients(first, count):
        conduct, open_, east, north = (ext[f, first : first + count + 2] for f in range(4))

        def leave_enter(near, near_open, far, far_open, flow):
            diffuse = jnp.sqrt(near * far)
            opened = near_open * far_open
            return (
                diffuse + opened * jnp.maximum(flow, 0.0),
                diffuse - opened * jnp.minimum(flow, 0.0),
            )

        mid = slice(1, count + 1)
        c, o = conduct[mid], open_[mid]
        c_next = pltpu.roll(c, width - 1, 1) * not_last
        o_next = pltpu.roll(o, width - 1, 1) * not_last
        out_e, in_e = leave_enter(c, o, c_next, o_next, east[mid])
        out_w = pltpu.roll(out_e, 1, 1) * not_first
        in_w = pltpu.roll(in_e, 1, 1) * not_first
        out_n, in_n = leave_enter(
            conduct[: count + 1], open_[: count + 1], conduct[1:], open_[1:], north[: count + 1]
        )
        where = slice(first + 1, first + 1 + count)
        coef[0, where] = o * (1.0 - out_e - in_w - out_n[1:] - in_n[:-1])
        coef[1, where] = o * in_e
        coef[2, where] = o * out_w
        coef[3, where] = o * in_n[1:]
        coef[4, where] = o * out_n[:-1]

    for first in range(0, rows, 8):
        coefficients(BASE - 1 + first, 8)
    coefficients(BASE - 2, 1)
    coefficients(BASE + rows - 1, 1)

    def stencil(source, at, row):
        def c(i):
            return jnp.broadcast_to(coef[i, pl.ds(row + BASE, 1), :], (OWN, width))

        here = source[at]
        return (
            c(0) * here
            + c(1) * pltpu.roll(here, width - 1, 1)
            + c(2) * pltpu.roll(here, 1, 1)
            + c(3) * source[at + 1]
            + c(4) * source[at - 1]
        )

    def first_step(i, carry):
        middle[i] = stencil(padded, i + 1, i - 1)
        return carry

    def second_step(i, carry):
        r = 2 * i
        pair = [stencil(middle, r + 1 + q, r + q) for q in range(2)]
        for q in range(2):
            forecast[r + q] = pair[q]
        value = jnp.concatenate(pair, 0)
        high = value.astype(BF16)
        rest = value - high.astype(F32)
        middle_part, low = split(rest)
        spot = pl.ds(pl.multiple_of(i * 2 * OWN, 2 * OWN), 2 * OWN)
        parts[0, spot] = high
        parts[1, spot] = middle_part
        parts[2, spot] = low
        return carry

    lax.fori_loop(0, rows + 2, first_step, 0, unroll=2)
    lax.fori_loop(0, rows // 2, second_step, 0)

    swaps = []
    for chunk in range(chunks):
        for d in range(1, n_mem):
            t = mem_of(d)
            swaps.append(
                pltpu.make_async_remote_copy(
                    src_ref=forecast.at[
                        pl.ds(chunk * rb, rb), :, pl.ds(pl.multiple_of(t * LANES, LANES), LANES)
                    ],
                    dst_ref=states.at[
                        pl.ds(chunk * rb, rb), pl.ds(pl.multiple_of(z * OWN, OWN), OWN), :
                    ],
                    send_sem=swap_send.at[chunk * n_mem + d],
                    recv_sem=swap_recv.at[chunk * n_mem + d],
                    device_id=(s, t),
                    device_id_type=MESH,
                )
            )
    for copy in swaps:
        copy.start()
    states[:, pl.ds(pl.multiple_of(z * OWN, OWN), OWN), :] = forecast[
        :, :, pl.ds(pl.multiple_of(z * LANES, LANES), LANES)
    ]

    per_batch = nobs // LANES

    def pick_batch(b, carry):
        line = line_of[pl.ds(b, 1), :]
        chosen_column = column_of[b]
        tracer = jnp.zeros((OWN, nobs), F32)
        for part in range(3):
            tracer_part = quick(parts[part], chosen_column).reshape(rows, OWN, nobs)
            for r in range(rows):
                tracer = tracer + jnp.where(line == r, tracer_part[r], 0.0)
        sea_part = quick(sea[...], chosen_column)
        at_row = lax.broadcasted_iota(jnp.int32, (rows, nobs), 0)
        found = jnp.sum(jnp.where(line == at_row, sea_part, 0.0), axis=0, keepdims=True)
        for q in range(per_batch):
            lanes = slice(LANES * q, LANES * (q + 1))
            picked[b * per_batch + q, 0:OWN] = tracer[:, lanes]
            picked[b * per_batch + q, OWN : 2 * OWN] = jnp.broadcast_to(
                found[:, lanes], (OWN, LANES)
            )
        return carry

    lax.fori_loop(0, batches, pick_batch, 0)

    reduces = []
    for d in range(1, n_slab):
        t = slab_of(d)
        reduces.append(
            pltpu.make_async_remote_copy(
                src_ref=picked.at[lax.rem(t, n_piece)],
                dst_ref=reduce_buf.at[d],
                send_sem=reduce_send.at[d],
                recv_sem=reduce_recv.at[d],
                device_id=(t, z),
                device_id_type=MESH,
            )
        )
    for copy in reduces:
        copy.start()
    total = picked[mine]
    for d, copy in enumerate(reduces, 1):
        copy.wait_recv()
        total = total + reduce_buf[d]
    piece[...] = total

    own_rows = pl.ds(pl.multiple_of(z * OWN, OWN), OWN)
    rings = []
    for d in range(1, n_mem):
        rings.append(
            pltpu.make_async_remote_copy(
                src_ref=piece.at[pl.ds(0, OWN)],
                dst_ref=gathered.at[own_rows],
                send_sem=ring_send.at[d],
                recv_sem=ring_recv.at[d],
                device_id=(s, mem_of(d)),
                device_id_type=MESH,
            )
        )
    for copy in rings:
        copy.start()
    gathered[own_rows] = total[0:OWN]
    gathered[members : members + OWN] = total[OWN : 2 * OWN]
    for copy in rings:
        copy.wait_recv()

    own_lanes = pl.ds(pl.multiple_of(mine * LANES, LANES), LANES)
    shares = []
    for d in range(1, n_piece):
        shares.append(
            pltpu.make_async_remote_copy(
                src_ref=gathered,
                dst_ref=site_cols.at[:, own_lanes],
                send_sem=share_send.at[d],
                recv_sem=share_recv.at[d],
                device_id=(piece_of(d), z),
                device_id_type=MESH,
            )
        )
    for copy in shares:
        copy.start()
    site_cols[:, own_lanes] = gathered[...]
    for copy in shares:
        copy.wait_recv()

    eye = (
        lax.broadcasted_iota(jnp.int32, (members, 2 * members), 0)
        == lax.broadcasted_iota(jnp.int32, (members, 2 * members), 1)
    ).astype(F32)
    for b in range(batches):
        now = slice(nobs * b, nobs * (b + 1))
        priors = site_cols[0:members, now]
        deviations = priors - jnp.mean(priors, axis=0, keepdims=True)
        inverse_var = 1.0 / var_ref[b : b + 1]
        misfit = base_misfit[b] - priors
        system = contract(
            deviations * inverse_var, jnp.concatenate([deviations, misfit], 0), (1, 1)
        ) + eye * (members - 1.0)
        solved = solve_spd(system)
        weights = (misfit - contract(solved, deviations, (0, 0))) * (
            inverse_var * (1.0 / (members - 1))
        )
        high, low = split(deviations.T)
        dcat[b] = jnp.concatenate([high, high, low], 1)
        high, low = split(weights)
        wcat[b] = jnp.concatenate([high, low], 0)
        if b < batches - 1:
            rest = slice(nobs * (b + 1), total_obs)
            values = site_cols[0:members, rest]
            anomalies = values - jnp.mean(values, axis=0, keepdims=True)
            covariance = contract(deviations, anomalies, (0, 0))
            site_cols[0:members, rest] = (
                values
                + contract(weights, tapers[b, :, rest] * covariance, (1, 0))
                * site_cols[members : members + 1, rest]
            )

    for chunk in range(chunks):
        for copy in swaps[chunk * (n_mem - 1) : (chunk + 1) * (n_mem - 1)]:
            copy.wait_recv()
        first = chunk * rb
        wet_here = jnp.concatenate([wet_cols[first + q : first + q + 1] for q in range(rb)], 1)
        here = jnp.concatenate([states[first + q] for q in range(rb)], 1)

        def assimilate(b, here):
            anomalies = here - jnp.mean(here, axis=0, keepdims=True)
            high, low = split(anomalies)
            covariance = quick(dcat[b], jnp.concatenate([high, low, high], 0))
            taper = []
            for q in range(rb):
                gap = row_site[b] - float(first + q)
                taper.append(jnp.exp(-rate * (gap * gap)) * column_taper[b])
            high, low = split(covariance * jnp.concatenate(taper, 1))
            both = quick(wcat[b], high)
            change = both[:members] + both[members:] + quick(wcat[b, 0:members], low)
            return here + change * wet_here

        here = lax.fori_loop(0, batches, assimilate, here)
        for q in range(rb):
            out_ref[pl.ds(first + q, members, stride=rows), :] = here[
                :, LANES * q : LANES * (q + 1)
            ]

    for copy in swaps + reduces + rings + shares:
        copy.wait_send()


def geometry_of(mesh_shape, rows, batches, nobs):
    n_piece = batches * nobs // LANES
    return mesh_shape["slab"], mesh_shape["mem"], n_piece, min(16, rows // 2)


def on_device(
    geometry,
    prior_concentrations,
    kappa,
    east_face_transport,
    v_north,
    land,
    obs_owner,
    obs_offset,
    obs_value,
    obs_var,
    obs_noise,
):
    n_slab, n_mem, n_piece, rb = geometry
    own, rows, width = prior_concentrations.shape
    batches, nobs = obs_value.shape
    members = own * n_mem
    chunks = rows // rb
    tall = rows + 2 * BASE
    vmem = pl.BlockSpec(memory_space=pltpu.VMEM)
    smem = pl.BlockSpec(memory_space=pltpu.SMEM)
    dma = pltpu.SemaphoreType.DMA
    out = pl.pallas_call(
        functools.partial(kernel, geometry),
        out_shape=jax.ShapeDtypeStruct((members * rows, LANES), F32),
        in_specs=[vmem] * 5 + [smem] + [vmem] * 4,
        out_specs=vmem,
        scratch_shapes=[
            pltpu.VMEM((rows + 4, own, width), F32),
            pltpu.VMEM((rows + 2, own, width), F32),
            pltpu.VMEM((rows, own, width), F32),
            pltpu.VMEM((rows, members, LANES), F32),
            pltpu.VMEM((2, 8, width), F32),
            pltpu.VMEM((2, 8, width), F32),
            pltpu.VMEM((4, tall, width), F32),
            pltpu.VMEM((5, tall, width), F32),
            pltpu.VMEM((3, rows * own, width), BF16),
            pltpu.VMEM((batches, width, nobs), BF16),
            pltpu.VMEM((batches, nobs), jnp.int32),
            pltpu.VMEM((rows, width), BF16),
            pltpu.VMEM((n_piece, 2 * own, LANES), F32),
            pltpu.VMEM((n_slab, 2 * own, LANES), F32),
            pltpu.VMEM((2 * own, LANES), F32),
            pltpu.VMEM((members + own, LANES), F32),
            pltpu.VMEM((2 * batches, nobs), F32),
            pltpu.VMEM((batches - 1, nobs, batches * nobs), F32),
            pltpu.VMEM((batches, members, nobs), F32),
            pltpu.VMEM((batches, nobs, 3 * members), BF16),
            pltpu.VMEM((batches, 2 * members, nobs), BF16),
            pltpu.VMEM((batches, nobs, LANES), F32),
            pltpu.VMEM((batches, nobs, LANES), F32),
            pltpu.VMEM((rows, LANES), F32),
            pltpu.VMEM((members + own, batches * nobs), F32),
            dma((4,)),
            dma((4,)),
            dma((n_slab,)),
            dma((n_slab,)),
            dma((n_mem,)),
            dma((n_mem,)),
            dma((n_piece,)),
            dma((n_piece,)),
            dma((chunks * n_mem,)),
            dma((chunks * n_mem,)),
        ],
        compiler_params=pltpu.CompilerParams(
            collective_id=0, has_side_effects=True, vmem_limit_bytes=48 << 20
        ),
    )(
        prior_concentrations,
        kappa,
        east_face_transport,
        v_north,
        land,
        obs_owner,
        obs_offset,
        obs_value,
        obs_var,
        obs_noise,
    )
    return out.reshape(members, rows, LANES)


def solution(mesh):
    placed = (
        P("mem", "slab", None),
        P("slab", None),
        P("slab", None),
        P("slab", None),
        P("slab", None),
        P(),
        P(),
        P(),
        P(),
        P(),
    )

    def whole(*arguments):
        prior, value = arguments[0], arguments[7]
        rows = prior.shape[1] // mesh.shape["slab"]
        geometry = geometry_of(mesh.shape, rows, *value.shape)
        return jax.shard_map(
            functools.partial(on_device, geometry),
            mesh=mesh,
            in_specs=placed,
            out_specs=P(None, "slab", "mem"),
            check_vma=False,
        )(*arguments)

    return whole
```

```python
import functools
import math

import jax
import jax.numpy as jnp
from jax import lax
from jax.experimental import pallas as pl
from jax.experimental.pallas import tpu as pltpu
from jax.sharding import PartitionSpec as P

F32 = jnp.float32
BF16 = jnp.bfloat16
PRECISE = lax.Precision.HIGHEST
MESH = pl.DeviceIdType.MESH
LANES = 128
OWN = 8
EARLY = 1
BASE = 8


def contract(a, b, dims):
    return lax.dot_general(
        a, b, ((dims[:1], dims[1:]), ((), ())), precision=PRECISE, preferred_element_type=F32
    )


def quick(a, b):
    return jnp.dot(a, b, preferred_element_type=F32)


def split(x):
    high = x.astype(BF16)
    return high, (x - high.astype(F32)).astype(BF16)


def solve_spd(system):
    rows, lanes = system.shape
    at = lax.broadcasted_iota(jnp.int32, (8, lanes), 0)

    def wide(x):
        return jnp.broadcast_to(x, (8, lanes))

    def block(_, parts):
        head, others = parts[0], parts[1:]
        columns = [wide(head[:, k : k + 1]) for k in range(8)]
        factors = [[wide(p[:, k : k + 1]) for k in range(8)] for p in others]
        for k in range(8):
            inverse = 1.0 / wide(columns[k][k : k + 1])
            pivot = wide(head[k : k + 1]) * inverse
            head = jnp.where(at == k, pivot, head - columns[k] * pivot)
            for q in range(k + 1, 8):
                entry = wide(columns[q][k : k + 1]) * inverse
                columns[q] = jnp.where(at == k, entry, columns[q] - columns[k] * entry)
        pivots = [wide(head[k : k + 1]) for k in range(8)]
        parts = []
        for p, f in zip(others, factors):
            terms = [f[k] * pivots[k] for k in range(8)]
            while len(terms) > 1:
                terms = [x + y for x, y in zip(terms[::2], terms[1::2])]
            parts.append(p - terms[0])
        return tuple(pltpu.roll(p, lanes - 8, 1) for p in parts + [head])

    parts = tuple(system[8 * i : 8 * i + 8] for i in range(rows // 8))
    parts = lax.fori_loop(0, rows // 8, block, parts)
    return jnp.concatenate(parts, 0)[:, :rows]


def kernel(
    geometry,
    prior_hbm,
    kappa_hbm,
    east_hbm,
    north_hbm,
    land_hbm,
    owner_ref,
    offset_hbm,
    value_hbm,
    var_hbm,
    noise_hbm,
    out_ref,
    prior_ref,
    kappa_ref,
    east_ref,
    north_ref,
    land_ref,
    offset_ref,
    value_ref,
    var_ref,
    noise_ref,
    padded,
    middle,
    forecast,
    states,
    stat_send,
    stat_recv,
    ext,
    coef,
    parts,
    column_of,
    line_of,
    sea,
    picked,
    reduce_buf,
    piece,
    gathered,
    sites,
    tapers,
    base_misfit,
    dcat,
    wcat,
    column_taper,
    row_site,
    wet_cols,
    site_cols,
    stage_sem,
    halo_send,
    halo_recv,
    reduce_send,
    reduce_recv,
    ring_send,
    ring_recv,
    share_send,
    share_recv,
    swap_send,
    swap_recv,
):
    n_slab, n_mem, n_piece, rb = geometry
    rows = kappa_ref.shape[0]
    width = kappa_ref.shape[1]
    members = OWN * n_mem
    batches, nobs = var_ref.shape
    total_obs = batches * nobs
    chunks = rows // rb
    extent = rows * n_slab // 2
    rate = 0.5 / (extent * extent)

    s = lax.axis_index("slab")
    z = lax.axis_index("mem")
    mine = lax.rem(s, n_piece)

    def slab_of(d):
        return lax.rem(s + d, n_slab)

    def mem_of(d):
        return lax.rem(z + d, n_mem)

    def piece_of(d):
        return s - mine + lax.rem(mine + d, n_piece)

    staged = [
        pltpu.make_async_copy(source, target, stage_sem.at[i])
        for i, (source, target) in enumerate(
            (
                (kappa_hbm, kappa_ref),
                (east_hbm, east_ref),
                (north_hbm, north_ref),
                (land_hbm, land_ref),
                (prior_hbm, prior_ref),
                (offset_hbm, offset_ref),
                (value_hbm, value_ref),
                (var_hbm, var_ref),
                (noise_hbm, noise_ref),
            )
        )
    ]
    for copy in staged:
        copy.start()

    barrier = pltpu.get_barrier_semaphore()
    for d in range(1, n_slab):
        pl.semaphore_signal(barrier, inc=1, device_id=(slab_of(d), z), device_id_type=MESH)
    for d in range(1, n_mem):
        pl.semaphore_signal(barrier, inc=1, device_id=(s, mem_of(d)), device_id_type=MESH)

    def fill(r):
        tile = prior_ref[:, pl.ds(r, 8), :]
        padded[pl.ds(r + 2, 8)] = jnp.swapaxes(tile, 0, 1)

    for copy in staged[:5]:
        copy.wait()
    wet = land_ref[...].astype(F32)
    ext[0, BASE : BASE + rows] = wet * kappa_ref[...]
    ext[1, BASE : BASE + rows] = wet
    ext[2, BASE : BASE + rows] = east_ref[...]
    ext[3, BASE : BASE + rows] = north_ref[...]
    for side, first in ((0, BASE), (1, BASE + rows - 2)):
        for field in range(4):
            stat_send[side, 2 * field : 2 * field + 2] = ext[field, first : first + 2]
    fill(0)
    fill(rows - 8)

    pl.semaphore_wait(barrier, n_slab - 1 + n_mem - 1)

    halo = []
    for side, (d, src, dst) in enumerate(
        ((n_slab - 1, 2, rows + 2), (1, rows, 0))
    ):
        target = (slab_of(d), z)
        halo.append(
            pltpu.make_async_remote_copy(
                src_ref=stat_send.at[side],
                dst_ref=stat_recv.at[side],
                send_sem=halo_send.at[2 * side],
                recv_sem=halo_recv.at[2 * side],
                device_id=target,
                device_id_type=MESH,
            )
        )
        halo.append(
            pltpu.make_async_remote_copy(
                src_ref=padded.at[pl.ds(src, 2)],
                dst_ref=padded.at[pl.ds(dst, 2)],
                send_sem=halo_send.at[2 * side + 1],
                recv_sem=halo_recv.at[2 * side + 1],
                device_id=target,
                device_id_type=MESH,
            )
        )
    for copy in halo:
        copy.start()

    def fill_rest(i, carry):
        fill(pl.multiple_of(8 * i, 8))
        return carry

    lax.fori_loop(1, rows // 8 - 1, fill_rest, 0)

    for copy in staged[5:]:
        copy.wait()
    offsets = offset_ref[...]
    batch_at = lax.broadcasted_iota(jnp.int32, offsets.shape, 0)
    owner_rows = jnp.zeros(offsets.shape, jnp.int32)
    for b in range(batches):
        owner_rows = jnp.where(batch_at == b, owner_ref[b] * rows, owner_rows)
    site_row = (owner_rows + offsets // width).astype(F32)
    site_col = (offsets % width).astype(F32)
    sites[0:batches] = site_row
    sites[batches : 2 * batches] = site_col
    line_of[...] = jnp.where(owner_rows == s * rows, offsets // width, -1)
    for b in range(batches):
        column = (offsets % width)[b : b + 1]
        for first in range(0, width, nobs):
            at = lax.broadcasted_iota(jnp.int32, (nobs, nobs), 0) + first
            column_of[b, first : first + nobs] = (at == column).astype(F32).astype(BF16)
    sea[...] = wet.astype(BF16)
    wet_cols[...] = land_ref[:, pl.ds(pl.multiple_of(z * LANES, LANES), LANES)].astype(F32)

    for copy in halo:
        copy.wait()

    low_ok = (s > 0).astype(F32)
    high_ok = (s < n_slab - 1).astype(F32)
    for field in range(4):
        ext[field, BASE - 2 : BASE] = stat_recv[1, 2 * field : 2 * field + 2] * low_ok
        ext[field, BASE + rows : BASE + rows + 2] = (
            stat_recv[0, 2 * field : 2 * field + 2] * high_ok
        )

    tall = ext.shape[1]
    lane = lax.broadcasted_iota(jnp.int32, (1, width), 1)
    not_last = (lane < width - 1).astype(F32)
    not_first = (lane > 0).astype(F32)

    def coefficients(first, count):
        conduct, open_, east, north = (ext[f, first : first + count + 2] for f in range(4))

        def leave_enter(near, near_open, far, far_open, flow):
            diffuse = jnp.sqrt(near * far)
            opened = near_open * far_open
            return (
                diffuse + opened * jnp.maximum(flow, 0.0),
                diffuse - opened * jnp.minimum(flow, 0.0),
            )

        mid = slice(1, count + 1)
        c, o = conduct[mid], open_[mid]
        c_next = pltpu.roll(c, width - 1, 1) * not_last
        o_next = pltpu.roll(o, width - 1, 1) * not_last
        out_e, in_e = leave_enter(c, o, c_next, o_next, east[mid])
        out_w = pltpu.roll(out_e, 1, 1) * not_first
        in_w = pltpu.roll(in_e, 1, 1) * not_first
        out_n, in_n = leave_enter(
            conduct[: count + 1], open_[: count + 1], conduct[1:], open_[1:], north[: count + 1]
        )
        where = slice(first + 1, first + 1 + count)
        coef[0, where] = o * (1.0 - out_e - in_w - out_n[1:] - in_n[:-1])
        coef[1, where] = o * in_e
        coef[2, where] = o * out_w
        coef[3, where] = o * in_n[1:]
        coef[4, where] = o * out_n[:-1]

    for first in range(0, rows, 8):
        coefficients(BASE - 1 + first, 8)
    coefficients(BASE - 2, 1)
    coefficients(BASE + rows - 1, 1)

    def stencil(source, at, row):
        def c(i):
            return jnp.broadcast_to(coef[i, pl.ds(row + BASE, 1), :], (OWN, width))

        here = source[at]
        return (
            c(0) * here
            + c(1) * pltpu.roll(here, width - 1, 1)
            + c(2) * pltpu.roll(here, 1, 1)
            + c(3) * source[at + 1]
            + c(4) * source[at - 1]
        )

    def first_step(i, carry):
        middle[i] = stencil(padded, i + 1, i - 1)
        return carry

    def second_step(i, carry):
        r = 2 * i
        pair = [stencil(middle, r + 1 + q, r + q) for q in range(2)]
        for q in range(2):
            forecast[r + q] = pair[q]
        value = jnp.concatenate(pair, 0)
        high = value.astype(BF16)
        rest = value - high.astype(F32)
        middle_part, low = split(rest)
        spot = pl.ds(pl.multiple_of(i * 2 * OWN, 2 * OWN), 2 * OWN)
        parts[0, spot] = high
        parts[1, spot] = middle_part
        parts[2, spot] = low
        return carry

    swaps = []
    for chunk in range(chunks):
        done = chunk * rb + 2 if chunk else 0
        lax.fori_loop(done, (chunk + 1) * rb + 2, first_step, 0, unroll=2)
        lax.fori_loop(chunk * rb // 2, (chunk + 1) * rb // 2, second_step, 0)
        for d in range(1, n_mem):
            t = mem_of(d)
            swaps.append(
                pltpu.make_async_remote_copy(
                    src_ref=forecast.at[
                        pl.ds(chunk * rb, rb), :, pl.ds(pl.multiple_of(t * LANES, LANES), LANES)
                    ],
                    dst_ref=states.at[
                        pl.ds(chunk * rb, rb), pl.ds(pl.multiple_of(z * OWN, OWN), OWN), :
                    ],
                    send_sem=swap_send.at[chunk * n_mem + d],
                    recv_sem=swap_recv.at[chunk * n_mem + d],
                    device_id=(s, t),
                    device_id_type=MESH,
                )
            )
        if chunk < EARLY:
            for copy in swaps[chunk * (n_mem - 1) :]:
                copy.start()
    states[:, pl.ds(pl.multiple_of(z * OWN, OWN), OWN), :] = forecast[
        :, :, pl.ds(pl.multiple_of(z * LANES, LANES), LANES)
    ]

    per_batch = nobs // LANES

    def pick_batch(b, carry):
        line = line_of[pl.ds(b, 1), :]
        chosen_column = column_of[b]
        tracer = jnp.zeros((OWN, nobs), F32)
        for part in range(3):
            tracer_part = quick(parts[part], chosen_column).reshape(rows, OWN, nobs)
            for r in range(rows):
                tracer = tracer + jnp.where(line == r, tracer_part[r], 0.0)
        sea_part = quick(sea[...], chosen_column)
        at_row = lax.broadcasted_iota(jnp.int32, (rows, nobs), 0)
        found = jnp.sum(jnp.where(line == at_row, sea_part, 0.0), axis=0, keepdims=True)
        for q in range(per_batch):
            lanes = slice(LANES * q, LANES * (q + 1))
            picked[b * per_batch + q, 0:OWN] = tracer[:, lanes]
            picked[b * per_batch + q, OWN : 2 * OWN] = jnp.broadcast_to(
                found[:, lanes], (OWN, LANES)
            )
        return carry

    lax.fori_loop(0, batches, pick_batch, 0)

    reduces = []
    for d in range(1, n_slab):
        t = slab_of(d)
        reduces.append(
            pltpu.make_async_remote_copy(
                src_ref=picked.at[lax.rem(t, n_piece)],
                dst_ref=reduce_buf.at[d],
                send_sem=reduce_send.at[d],
                recv_sem=reduce_recv.at[d],
                device_id=(t, z),
                device_id_type=MESH,
            )
        )
    for copy in reduces:
        copy.start()
    flipped = sites[...].T
    for b in range(batches - 1):
        row_j = flipped[:, b : b + 1]
        col_j = flipped[:, batches + b : batches + b + 1]
        for later in range(b + 1, batches):
            g_row = row_j - sites[later : later + 1]
            g_col = col_j - sites[batches + later : batches + later + 1]
            tapers[b, :, nobs * later : nobs * (later + 1)] = jnp.exp(
                -rate * (g_row * g_row + g_col * g_col)
            )

    total = picked[mine]
    for d, copy in enumerate(reduces, 1):
        copy.wait_recv()
        total = total + reduce_buf[d]
    piece[...] = total

    own_rows = pl.ds(pl.multiple_of(z * OWN, OWN), OWN)
    rings = []
    for d in range(1, n_mem):
        rings.append(
            pltpu.make_async_remote_copy(
                src_ref=piece.at[pl.ds(0, OWN)],
                dst_ref=gathered.at[own_rows],
                send_sem=ring_send.at[d],
                recv_sem=ring_recv.at[d],
                device_id=(s, mem_of(d)),
                device_id_type=MESH,
            )
        )
    for copy in rings:
        copy.start()
    gathered[own_rows] = total[0:OWN]
    gathered[members : members + OWN] = total[OWN : 2 * OWN]
    row0 = (s * rows).astype(F32)
    col0 = (z * LANES).astype(F32)
    columns = lax.broadcasted_iota(jnp.int32, (1, LANES), 1).astype(F32) + col0
    for b in range(batches):
        gap = flipped[:, batches + b : batches + b + 1] - columns
        column_taper[b] = jnp.exp(-rate * (gap * gap))
        row_site[b] = jnp.broadcast_to(flipped[:, b : b + 1], (nobs, LANES)) - row0
        base_misfit[b] = value_ref[b : b + 1] + jnp.sqrt(var_ref[b : b + 1]) * noise_ref[b]
    for copy in rings:
        copy.wait_recv()

    for copy in swaps[EARLY * (n_mem - 1) :]:
        copy.start()

    own_lanes = pl.ds(pl.multiple_of(mine * LANES, LANES), LANES)
    shares = []
    for d in range(1, n_piece):
        shares.append(
            pltpu.make_async_remote_copy(
                src_ref=gathered,
                dst_ref=site_cols.at[:, own_lanes],
                send_sem=share_send.at[d],
                recv_sem=share_recv.at[d],
                device_id=(piece_of(d), z),
                device_id_type=MESH,
            )
        )
    for copy in shares:
        copy.start()
    site_cols[:, own_lanes] = gathered[...]
    for copy in shares:
        copy.wait_recv()

    eye = (
        lax.broadcasted_iota(jnp.int32, (members, 2 * members), 0)
        == lax.broadcasted_iota(jnp.int32, (members, 2 * members), 1)
    ).astype(F32)
    for b in range(batches):
        now = slice(nobs * b, nobs * (b + 1))
        priors = site_cols[0:members, now]
        deviations = priors - jnp.mean(priors, axis=0, keepdims=True)
        inverse_var = 1.0 / var_ref[b : b + 1]
        misfit = base_misfit[b] - priors
        system = contract(
            deviations * inverse_var, jnp.concatenate([deviations, misfit], 0), (1, 1)
        ) + eye * (members - 1.0)
        solved = solve_spd(system)
        weights = (misfit - contract(solved, deviations, (0, 0))) * (
            inverse_var * (1.0 / (members - 1))
        )
        high, low = split(deviations.T)
        dcat[b] = jnp.concatenate([high, high, low], 1)
        high, low = split(weights)
        wcat[b] = jnp.concatenate([high, low], 0)
        if b < batches - 1:
            rest = slice(nobs * (b + 1), total_obs)
            values = site_cols[0:members, rest]
            anomalies = values - jnp.mean(values, axis=0, keepdims=True)
            covariance = contract(deviations, anomalies, (0, 0))
            site_cols[0:members, rest] = (
                values
                + contract(weights, tapers[b, :, rest] * covariance, (1, 0))
                * site_cols[members : members + 1, rest]
            )

    for chunk in range(chunks):
        for copy in swaps[chunk * (n_mem - 1) : (chunk + 1) * (n_mem - 1)]:
            copy.wait_recv()
        first = chunk * rb
        wet_here = jnp.concatenate(
            [wet_cols[first + q : first + q + 1] * math.exp(-rate * q * q) for q in range(rb)], 1
        )
        here = jnp.concatenate([states[first + q] for q in range(rb)], 1)

        def assimilate(b, here):
            anomalies = here - jnp.mean(here, axis=0, keepdims=True)
            high, low = split(anomalies)
            covariance = quick(dcat[b], jnp.concatenate([high, low, high], 0))
            gap = row_site[b] - float(first)
            step = jnp.exp((2.0 * rate) * gap)
            taper = jnp.exp(-rate * (gap * gap)) * column_taper[b]
            weighted = []
            for q in range(rb):
                weighted.append(covariance[:, LANES * q : LANES * (q + 1)] * taper)
                taper = taper * step
            high, low = split(jnp.concatenate(weighted, 1))
            both = quick(wcat[b], high)
            change = both[:members] + both[members:] + quick(wcat[b, 0:members], low)
            return here + change * wet_here

        here = lax.fori_loop(0, batches, assimilate, here)
        for q in range(rb):
            out_ref[pl.ds(first + q, members, stride=rows), :] = here[
                :, LANES * q : LANES * (q + 1)
            ]

    for copy in swaps + reduces + rings + shares:
        copy.wait_send()


def geometry_of(mesh_shape, rows, batches, nobs):
    n_piece = batches * nobs // LANES
    return mesh_shape["slab"], mesh_shape["mem"], n_piece, min(16, rows // 2)


def on_device(
    geometry,
    prior_concentrations,
    kappa,
    east_face_transport,
    v_north,
    land,
    obs_owner,
    obs_offset,
    obs_value,
    obs_var,
    obs_noise,
):
    n_slab, n_mem, n_piece, rb = geometry
    own, rows, width = prior_concentrations.shape
    batches, nobs = obs_value.shape
    members = own * n_mem
    chunks = rows // rb
    tall = rows + 2 * BASE
    vmem = pl.BlockSpec(memory_space=pltpu.VMEM)
    smem = pl.BlockSpec(memory_space=pltpu.SMEM)
    hbm = pl.BlockSpec(memory_space=pltpu.HBM)
    dma = pltpu.SemaphoreType.DMA
    out = pl.pallas_call(
        functools.partial(kernel, geometry),
        out_shape=jax.ShapeDtypeStruct((members * rows, LANES), F32),
        in_specs=[hbm] * 5 + [smem] + [hbm] * 4,
        out_specs=vmem,
        scratch_shapes=[
            pltpu.VMEM((own, rows, width), F32),
            pltpu.VMEM((rows, width), F32),
            pltpu.VMEM((rows, width), F32),
            pltpu.VMEM((rows, width), F32),
            pltpu.VMEM((rows, width), jnp.int32),
            pltpu.VMEM((batches, nobs), jnp.int32),
            pltpu.VMEM((batches, nobs), F32),
            pltpu.VMEM((batches, nobs), F32),
            pltpu.VMEM((batches, members, nobs), F32),
            pltpu.VMEM((rows + 4, own, width), F32),
            pltpu.VMEM((rows + 2, own, width), F32),
            pltpu.VMEM((rows, own, width), F32),
            pltpu.VMEM((rows, members, LANES), F32),
            pltpu.VMEM((2, 8, width), F32),
            pltpu.VMEM((2, 8, width), F32),
            pltpu.VMEM((4, tall, width), F32),
            pltpu.VMEM((5, tall, width), F32),
            pltpu.VMEM((3, rows * own, width), BF16),
            pltpu.VMEM((batches, width, nobs), BF16),
            pltpu.VMEM((batches, nobs), jnp.int32),
            pltpu.VMEM((rows, width), BF16),
            pltpu.VMEM((n_piece, 2 * own, LANES), F32),
            pltpu.VMEM((n_slab, 2 * own, LANES), F32),
            pltpu.VMEM((2 * own, LANES), F32),
            pltpu.VMEM((members + own, LANES), F32),
            pltpu.VMEM((2 * batches, nobs), F32),
            pltpu.VMEM((batches - 1, nobs, batches * nobs), F32),
            pltpu.VMEM((batches, members, nobs), F32),
            pltpu.VMEM((batches, nobs, 3 * members), BF16),
            pltpu.VMEM((batches, 2 * members, nobs), BF16),
            pltpu.VMEM((batches, nobs, LANES), F32),
            pltpu.VMEM((batches, nobs, LANES), F32),
            pltpu.VMEM((rows, LANES), F32),
            pltpu.VMEM((members + own, batches * nobs), F32),
            dma((9,)),
            dma((4,)),
            dma((4,)),
            dma((n_slab,)),
            dma((n_slab,)),
            dma((n_mem,)),
            dma((n_mem,)),
            dma((n_piece,)),
            dma((n_piece,)),
            dma((chunks * n_mem,)),
            dma((chunks * n_mem,)),
        ],
        compiler_params=pltpu.CompilerParams(
            collective_id=0, has_side_effects=True, vmem_limit_bytes=60 << 20
        ),
    )(
        prior_concentrations,
        kappa,
        east_face_transport,
        v_north,
        land,
        obs_owner,
        obs_offset,
        obs_value,
        obs_var,
        jnp.swapaxes(obs_noise, 1, 2),
    )
    return out.reshape(members, rows, LANES)


def solution(mesh):
    placed = (
        P("mem", "slab", None),
        P("slab", None),
        P("slab", None),
        P("slab", None),
        P("slab", None),
        P(),
        P(),
        P(),
        P(),
        P(),
    )

    def whole(*arguments):
        prior, value = arguments[0], arguments[7]
        rows = prior.shape[1] // mesh.shape["slab"]
        geometry = geometry_of(mesh.shape, rows, *value.shape)
        return jax.shard_map(
            functools.partial(on_device, geometry),
            mesh=mesh,
            in_specs=placed,
            out_specs=P(None, "slab", "mem"),
            check_vma=False,
        )(*arguments)

    return whole
```

```python
import functools
import math

import jax
import jax.numpy as jnp
from jax import lax
from jax.experimental import pallas as pl
from jax.experimental.pallas import tpu as pltpu
from jax.sharding import PartitionSpec as P

F32 = jnp.float32
BF16 = jnp.bfloat16
PRECISE = lax.Precision.HIGHEST
MESH = pl.DeviceIdType.MESH
LANES = 128
OWN = 8
EARLY = 4
BASE = 8


def contract(a, b, dims):
    return lax.dot_general(
        a, b, ((dims[:1], dims[1:]), ((), ())), precision=PRECISE, preferred_element_type=F32
    )


def quick(a, b):
    return jnp.dot(a, b, preferred_element_type=F32)


def split(x):
    high = x.astype(BF16)
    return high, (x - high.astype(F32)).astype(BF16)


def solve_spd(system):
    rows, lanes = system.shape
    at = lax.broadcasted_iota(jnp.int32, (8, lanes), 0)

    def wide(x):
        return jnp.broadcast_to(x, (8, lanes))

    def block(_, parts):
        head, others = parts[0], parts[1:]
        columns = [wide(head[:, k : k + 1]) for k in range(8)]
        factors = [[wide(p[:, k : k + 1]) for k in range(8)] for p in others]
        for k in range(0, 8, 2):
            p, v = (wide(columns[k][r : r + 1]) for r in (k, k + 1))
            u, w = (wide(columns[k + 1][r : r + 1]) for r in (k, k + 1))
            inverse = 1.0 / (p * w - u * v)
            p, u, v, w = p * inverse, u * inverse, v * inverse, w * inverse

            def eliminate(x):
                upper, lower = wide(x[k : k + 1]), wide(x[k + 1 : k + 2])
                first = w * upper - u * lower
                second = p * lower - v * upper
                x = x - (columns[k] * first + columns[k + 1] * second)
                return jnp.where(at == k, first, jnp.where(at == k + 1, second, x))

            head = eliminate(head)
            for q in range(k + 2, 8):
                columns[q] = eliminate(columns[q])
        pivots = [wide(head[k : k + 1]) for k in range(8)]
        parts = []
        for p, f in zip(others, factors):
            terms = [f[k] * pivots[k] for k in range(8)]
            while len(terms) > 1:
                terms = [x + y for x, y in zip(terms[::2], terms[1::2])]
            parts.append(p - terms[0])
        return tuple(pltpu.roll(p, lanes - 8, 1) for p in parts + [head])

    parts = tuple(system[8 * i : 8 * i + 8] for i in range(rows // 8))
    parts = lax.fori_loop(0, rows // 8, block, parts)
    return jnp.concatenate(parts, 0)[:, :rows]


def kernel(
    geometry,
    prior_hbm,
    kappa_hbm,
    east_hbm,
    north_hbm,
    land_hbm,
    owner_ref,
    offset_hbm,
    value_hbm,
    var_hbm,
    noise_hbm,
    out_ref,
    prior_ref,
    kappa_ref,
    east_ref,
    north_ref,
    land_ref,
    offset_ref,
    value_ref,
    var_ref,
    noise_ref,
    padded,
    middle,
    forecast,
    states,
    stat_send,
    stat_recv,
    ext,
    coef,
    parts,
    column_of,
    line_of,
    sea,
    picked,
    reduce_buf,
    piece,
    gathered,
    sites,
    tapers,
    base_misfit,
    dcat,
    wcat,
    column_taper,
    row_site,
    wet_cols,
    site_cols,
    stage_sem,
    halo_send,
    halo_recv,
    reduce_send,
    reduce_recv,
    ring_send,
    ring_recv,
    share_send,
    share_recv,
    swap_send,
    swap_recv,
):
    n_slab, n_mem, n_piece, rb = geometry
    rows = kappa_ref.shape[0]
    width = kappa_ref.shape[1]
    members = OWN * n_mem
    batches, nobs = var_ref.shape
    total_obs = batches * nobs
    chunks = rows // rb
    extent = rows * n_slab // 2
    rate = 0.5 / (extent * extent)

    s = lax.axis_index("slab")
    z = lax.axis_index("mem")
    mine = lax.rem(s, n_piece)

    def slab_of(d):
        return lax.rem(s + d, n_slab)

    def mem_of(d):
        return lax.rem(z + d, n_mem)

    def piece_of(d):
        return s - mine + lax.rem(mine + d, n_piece)

    staged = [
        pltpu.make_async_copy(source, target, stage_sem.at[i])
        for i, (source, target) in enumerate(
            (
                (kappa_hbm, kappa_ref),
                (east_hbm, east_ref),
                (north_hbm, north_ref),
                (land_hbm, land_ref),
                (prior_hbm, prior_ref),
                (offset_hbm, offset_ref),
                (value_hbm, value_ref),
                (var_hbm, var_ref),
                (noise_hbm, noise_ref),
            )
        )
    ]
    for copy in staged:
        copy.start()

    barrier = pltpu.get_barrier_semaphore()
    for d in range(1, n_slab):
        pl.semaphore_signal(barrier, inc=1, device_id=(slab_of(d), z), device_id_type=MESH)
    for d in range(1, n_mem):
        pl.semaphore_signal(barrier, inc=1, device_id=(s, mem_of(d)), device_id_type=MESH)

    def fill(r):
        tile = prior_ref[:, pl.ds(r, 8), :]
        padded[pl.ds(r + 2, 8)] = jnp.swapaxes(tile, 0, 1)

    for copy in staged[:5]:
        copy.wait()
    wet = land_ref[...].astype(F32)
    ext[0, BASE : BASE + rows] = wet * kappa_ref[...]
    ext[1, BASE : BASE + rows] = wet
    ext[2, BASE : BASE + rows] = east_ref[...]
    ext[3, BASE : BASE + rows] = north_ref[...]
    for side, first in ((0, BASE), (1, BASE + rows - 2)):
        for field in range(4):
            stat_send[side, 2 * field : 2 * field + 2] = ext[field, first : first + 2]
    fill(0)
    fill(rows - 8)

    pl.semaphore_wait(barrier, n_slab - 1 + n_mem - 1)

    halo = []
    for side, (d, src, dst) in enumerate(
        ((n_slab - 1, 2, rows + 2), (1, rows, 0))
    ):
        target = (slab_of(d), z)
        halo.append(
            pltpu.make_async_remote_copy(
                src_ref=stat_send.at[side],
                dst_ref=stat_recv.at[side],
                send_sem=halo_send.at[2 * side],
                recv_sem=halo_recv.at[2 * side],
                device_id=target,
                device_id_type=MESH,
            )
        )
        halo.append(
            pltpu.make_async_remote_copy(
                src_ref=padded.at[pl.ds(src, 2)],
                dst_ref=padded.at[pl.ds(dst, 2)],
                send_sem=halo_send.at[2 * side + 1],
                recv_sem=halo_recv.at[2 * side + 1],
                device_id=target,
                device_id_type=MESH,
            )
        )
    for copy in halo:
        copy.start()

    def fill_rest(i, carry):
        fill(pl.multiple_of(8 * i, 8))
        return carry

    lax.fori_loop(1, rows // 8 - 1, fill_rest, 0)

    for copy in staged[5:]:
        copy.wait()
    offsets = offset_ref[...]
    batch_at = lax.broadcasted_iota(jnp.int32, offsets.shape, 0)
    owner_rows = jnp.zeros(offsets.shape, jnp.int32)
    for b in range(batches):
        owner_rows = jnp.where(batch_at == b, owner_ref[b] * rows, owner_rows)
    site_row = (owner_rows + offsets // width).astype(F32)
    site_col = (offsets % width).astype(F32)
    sites[0:batches] = site_row
    sites[batches : 2 * batches] = site_col
    line_of[...] = jnp.where(owner_rows == s * rows, offsets // width, -1)
    for b in range(batches):
        column = (offsets % width)[b : b + 1]
        for first in range(0, width, nobs):
            at = lax.broadcasted_iota(jnp.int32, (nobs, nobs), 0) + first
            column_of[b, first : first + nobs] = (at == column).astype(F32).astype(BF16)
    sea[...] = wet.astype(BF16)
    wet_cols[...] = land_ref[:, pl.ds(pl.multiple_of(z * LANES, LANES), LANES)].astype(F32)

    tall = ext.shape[1]
    lane = lax.broadcasted_iota(jnp.int32, (1, width), 1)
    not_last = (lane < width - 1).astype(F32)
    not_first = (lane > 0).astype(F32)

    def coefficients(first, count):
        conduct, open_, east, north = (ext[f, first : first + count + 2] for f in range(4))

        def leave_enter(near, near_open, far, far_open, flow):
            diffuse = jnp.sqrt(near * far)
            opened = near_open * far_open
            return (
                diffuse + opened * jnp.maximum(flow, 0.0),
                diffuse - opened * jnp.minimum(flow, 0.0),
            )

        mid = slice(1, count + 1)
        c, o = conduct[mid], open_[mid]
        c_next = pltpu.roll(c, width - 1, 1) * not_last
        o_next = pltpu.roll(o, width - 1, 1) * not_last
        out_e, in_e = leave_enter(c, o, c_next, o_next, east[mid])
        out_w = pltpu.roll(out_e, 1, 1) * not_first
        in_w = pltpu.roll(in_e, 1, 1) * not_first
        out_n, in_n = leave_enter(
            conduct[: count + 1], open_[: count + 1], conduct[1:], open_[1:], north[: count + 1]
        )
        where = slice(first + 1, first + 1 + count)
        coef[0, where] = o * (1.0 - out_e - in_w - out_n[1:] - in_n[:-1])
        coef[1, where] = o * in_e
        coef[2, where] = o * out_w
        coef[3, where] = o * in_n[1:]
        coef[4, where] = o * out_n[:-1]


    def stencil(source, at, row):
        def c(i):
            return jnp.broadcast_to(coef[i, pl.ds(row + BASE, 1), :], (OWN, width))

        here = source[at]
        return (
            c(0) * here
            + c(1) * pltpu.roll(here, width - 1, 1)
            + c(2) * pltpu.roll(here, 1, 1)
            + c(3) * source[at + 1]
            + c(4) * source[at - 1]
        )

    def first_step(i, carry):
        middle[i] = stencil(padded, i + 1, i - 1)
        return carry

    def second_step(i, carry):
        r = 2 * i
        pair = [stencil(middle, r + 1 + q, r + q) for q in range(2)]
        for q in range(2):
            forecast[r + q] = pair[q]
        value = jnp.concatenate(pair, 0)
        high = value.astype(BF16)
        rest = value - high.astype(F32)
        middle_part, low = split(rest)
        spot = pl.ds(pl.multiple_of(i * 2 * OWN, 2 * OWN), 2 * OWN)
        parts[0, spot] = high
        parts[1, spot] = middle_part
        parts[2, spot] = low
        return carry

    swaps = {}

    def advance(chunk):
        start = 0 if chunk == 0 else chunk * rb + (0 if chunk == 1 else 2)
        stop = rb if chunk == 0 else (chunk + 1) * rb + 2
        lax.fori_loop(start, stop, first_step, 0, unroll=2)
        lax.fori_loop(chunk * rb // 2, (chunk + 1) * rb // 2, second_step, 0)
        for d in range(1, n_mem):
            t = mem_of(d)
            swaps[chunk, d] = pltpu.make_async_remote_copy(
                src_ref=forecast.at[
                    pl.ds(chunk * rb, rb), :, pl.ds(pl.multiple_of(t * LANES, LANES), LANES)
                ],
                dst_ref=states.at[
                    pl.ds(chunk * rb, rb), pl.ds(pl.multiple_of(z * OWN, OWN), OWN), :
                ],
                send_sem=swap_send.at[chunk * n_mem + d],
                recv_sem=swap_recv.at[chunk * n_mem + d],
                device_id=(s, t),
                device_id_type=MESH,
            )

    order = [*range(1, chunks - 1), 0, chunks - 1]
    steps = [(chunk, d) for chunk in order for d in range(1, n_mem)]
    early = EARLY * (n_mem - 1) // 4
    for first in range(8, rows - 8, 8):
        coefficients(BASE - 1 + first, 8)
    for chunk in order:
        if chunk == 0:
            for copy in halo:
                copy.wait()

            low_ok = (s > 0).astype(F32)
            high_ok = (s < n_slab - 1).astype(F32)
            for field in range(4):
                ext[field, BASE - 2 : BASE] = stat_recv[1, 2 * field : 2 * field + 2] * low_ok
                ext[field, BASE + rows : BASE + rows + 2] = (
                    stat_recv[0, 2 * field : 2 * field + 2] * high_ok
                )
            for first in (0, rows - 8):
                coefficients(BASE - 1 + first, 8)
            coefficients(BASE - 2, 1)
            coefficients(BASE + rows - 1, 1)
        advance(chunk)
        for step in steps[:early]:
            if step[0] == chunk:
                swaps[step].start()
    states[:, pl.ds(pl.multiple_of(z * OWN, OWN), OWN), :] = forecast[
        :, :, pl.ds(pl.multiple_of(z * LANES, LANES), LANES)
    ]

    per_batch = nobs // LANES

    def reduce_to(t):
        return pltpu.make_async_remote_copy(
            src_ref=picked.at[lax.rem(t, n_piece)],
            dst_ref=reduce_buf.at[s],
            send_sem=reduce_send.at[t],
            recv_sem=reduce_recv.at[s],
            device_id=(t, z),
            device_id_type=MESH,
        )

    def reduce_from(t):
        return pltpu.make_async_remote_copy(
            src_ref=picked.at[mine],
            dst_ref=reduce_buf.at[t],
            send_sem=reduce_send.at[t],
            recv_sem=reduce_recv.at[t],
            device_id=(t, z),
            device_id_type=MESH,
        )

    def pick_batch(b, carry):
        line = line_of[pl.ds(b, 1), :]
        chosen_column = column_of[b]
        tracer = jnp.zeros((OWN, nobs), F32)
        at_line = lax.broadcasted_iota(jnp.int32, (rows, OWN, nobs), 0) == line[None]
        for part in range(3):
            part_here = quick(parts[part], chosen_column).reshape(rows, OWN, nobs)
            tracer = tracer + jnp.sum(jnp.where(at_line, part_here, 0.0), axis=0)
        sea_part = quick(sea[...], chosen_column)
        at_row = lax.broadcasted_iota(jnp.int32, (rows, nobs), 0)
        found = jnp.sum(jnp.where(line == at_row, sea_part, 0.0), axis=0, keepdims=True)
        for q in range(per_batch):
            lanes = slice(LANES * q, LANES * (q + 1))
            picked[b * per_batch + q, 0:OWN] = tracer[:, lanes]
            picked[b * per_batch + q, OWN : 2 * OWN] = jnp.broadcast_to(
                found[:, lanes], (OWN, LANES)
            )
            for group in range(0, n_slab, n_piece):
                t = group + b * per_batch + q

                @pl.when(t != s)
                def _():
                    reduce_to(t).start()

        return carry

    lax.fori_loop(0, batches, pick_batch, 0)

    flipped = sites[...].T
    for b in range(batches - 1):
        row_j = flipped[:, b : b + 1]
        col_j = flipped[:, batches + b : batches + b + 1]
        for later in range(b + 1, batches):
            g_row = row_j - sites[later : later + 1]
            g_col = col_j - sites[batches + later : batches + later + 1]
            tapers[b, :, nobs * later : nobs * (later + 1)] = jnp.exp(
                -rate * (g_row * g_row + g_col * g_col)
            )

    total = picked[mine]
    for d in range(1, n_slab):
        reduce_from(slab_of(d)).wait_recv()
        total = total + reduce_buf[slab_of(d)]
    piece[...] = total

    own_rows = pl.ds(pl.multiple_of(z * OWN, OWN), OWN)
    rings = []
    for d in range(1, n_mem):
        rings.append(
            pltpu.make_async_remote_copy(
                src_ref=piece.at[pl.ds(0, OWN)],
                dst_ref=gathered.at[own_rows],
                send_sem=ring_send.at[d],
                recv_sem=ring_recv.at[d],
                device_id=(s, mem_of(d)),
                device_id_type=MESH,
            )
        )
    for copy in rings:
        copy.start()
    gathered[own_rows] = total[0:OWN]
    gathered[members : members + OWN] = total[OWN : 2 * OWN]
    row0 = (s * rows).astype(F32)
    col0 = (z * LANES).astype(F32)
    columns = lax.broadcasted_iota(jnp.int32, (1, LANES), 1).astype(F32) + col0
    for b in range(batches):
        gap = flipped[:, batches + b : batches + b + 1] - columns
        column_taper[b] = jnp.exp(-rate * (gap * gap))
        row_site[b] = jnp.broadcast_to(flipped[:, b : b + 1], (nobs, LANES)) - row0
        base_misfit[b] = value_ref[b : b + 1] + jnp.sqrt(var_ref[b : b + 1]) * noise_ref[b]
    for copy in rings:
        copy.wait_recv()

    for step in steps[early:]:
        swaps[step].start()

    own_lanes = pl.ds(pl.multiple_of(mine * LANES, LANES), LANES)
    shares = []
    for d in range(1, n_piece):
        shares.append(
            pltpu.make_async_remote_copy(
                src_ref=gathered,
                dst_ref=site_cols.at[:, own_lanes],
                send_sem=share_send.at[d],
                recv_sem=share_recv.at[mine],
                device_id=(piece_of(d), z),
                device_id_type=MESH,
            )
        )
    for copy in shares:
        copy.start()
    site_cols[:, own_lanes] = gathered[...]

    def wait_pieces(which):
        for p in which:

            @pl.when(p != mine)
            def _():
                pltpu.make_async_remote_copy(
                    src_ref=gathered,
                    dst_ref=site_cols.at[:, pl.ds(p * LANES, LANES)],
                    send_sem=share_send.at[p],
                    recv_sem=share_recv.at[p],
                    device_id=(piece_of(1), z),
                    device_id_type=MESH,
                ).wait_recv()


    eye = (
        lax.broadcasted_iota(jnp.int32, (members, 2 * members), 0)
        == lax.broadcasted_iota(jnp.int32, (members, 2 * members), 1)
    ).astype(F32)
    wait_pieces(range(per_batch))
    for b in range(batches):
        now = slice(nobs * b, nobs * (b + 1))
        priors = site_cols[0:members, now]
        deviations = priors - jnp.mean(priors, axis=0, keepdims=True)
        inverse_var = 1.0 / var_ref[b : b + 1]
        misfit = base_misfit[b] - priors
        system = contract(
            deviations * inverse_var, jnp.concatenate([deviations, misfit], 0), (1, 1)
        ) + eye * (members - 1.0)
        high, low = split(deviations.T)
        dcat[b] = jnp.concatenate([high, high, low], 1)
        solved = solve_spd(system)
        if b == 0:
            wait_pieces(range(per_batch, n_piece))
        weights = (misfit - contract(solved, deviations, (0, 0))) * (
            inverse_var * (1.0 / (members - 1))
        )
        high, low = split(weights)
        wcat[b] = jnp.concatenate([high, low], 0)
        if b < batches - 1:
            rest = slice(nobs * (b + 1), total_obs)
            values = site_cols[0:members, rest]
            anomalies = values - jnp.mean(values, axis=0, keepdims=True)
            high, low = split(anomalies)
            covariance = quick(dcat[b], jnp.concatenate([high, low, high], 0))
            high, low = split(tapers[b, :, rest] * covariance)
            both = quick(wcat[b], high)
            change = both[:members] + both[members:] + quick(wcat[b, 0:members], low)
            site_cols[0:members, rest] = (
                values + change * site_cols[members : members + 1, rest]
            )

    for chunk in order:
        for d in range(1, n_mem):
            swaps[chunk, d].wait_recv()
        first = chunk * rb
        wet_here = jnp.concatenate(
            [wet_cols[first + q : first + q + 1] * math.exp(-rate * q * q) for q in range(rb)], 1
        )
        here = jnp.concatenate([states[first + q] for q in range(rb)], 1)

        def assimilate(b, here):
            anomalies = here - jnp.mean(here, axis=0, keepdims=True)
            high, low = split(anomalies)
            covariance = quick(dcat[b], jnp.concatenate([high, low, high], 0))
            gap = row_site[b] - float(first)
            step = jnp.exp((2.0 * rate) * gap)
            taper = jnp.exp(-rate * (gap * gap)) * column_taper[b]
            weighted = []
            for q in range(rb):
                weighted.append(covariance[:, LANES * q : LANES * (q + 1)] * taper)
                taper = taper * step
            high, low = split(jnp.concatenate(weighted, 1))
            both = quick(wcat[b], high)
            change = both[:members] + both[members:] + quick(wcat[b, 0:members], low)
            return here + change * wet_here

        here = lax.fori_loop(0, batches, assimilate, here)
        for q in range(rb):
            out_ref[pl.ds(first + q, members, stride=rows), :] = here[
                :, LANES * q : LANES * (q + 1)
            ]

    for d in range(1, n_slab):
        reduce_from(slab_of(d)).wait_send()
    for copy in [*swaps.values(), *rings, *shares]:
        copy.wait_send()


def geometry_of(mesh_shape, rows, batches, nobs):
    n_piece = batches * nobs // LANES
    return mesh_shape["slab"], mesh_shape["mem"], n_piece, rows // 4


def on_device(
    geometry,
    prior_concentrations,
    kappa,
    east_face_transport,
    v_north,
    land,
    obs_owner,
    obs_offset,
    obs_value,
    obs_var,
    obs_noise,
):
    n_slab, n_mem, n_piece, rb = geometry
    own, rows, width = prior_concentrations.shape
    batches, nobs = obs_value.shape
    members = own * n_mem
    chunks = rows // rb
    tall = rows + 2 * BASE
    vmem = pl.BlockSpec(memory_space=pltpu.VMEM)
    smem = pl.BlockSpec(memory_space=pltpu.SMEM)
    hbm = pl.BlockSpec(memory_space=pltpu.HBM)
    dma = pltpu.SemaphoreType.DMA
    out = pl.pallas_call(
        functools.partial(kernel, geometry),
        out_shape=jax.ShapeDtypeStruct((members * rows, LANES), F32),
        in_specs=[hbm] * 5 + [smem] + [hbm] * 4,
        out_specs=vmem,
        scratch_shapes=[
            pltpu.VMEM((own, rows, width), F32),
            pltpu.VMEM((rows, width), F32),
            pltpu.VMEM((rows, width), F32),
            pltpu.VMEM((rows, width), F32),
            pltpu.VMEM((rows, width), jnp.int32),
            pltpu.VMEM((batches, nobs), jnp.int32),
            pltpu.VMEM((batches, nobs), F32),
            pltpu.VMEM((batches, nobs), F32),
            pltpu.VMEM((batches, members, nobs), F32),
            pltpu.VMEM((rows + 4, own, width), F32),
            pltpu.VMEM((rows + 2, own, width), F32),
            pltpu.VMEM((rows, own, width), F32),
            pltpu.VMEM((rows, members, LANES), F32),
            pltpu.VMEM((2, 8, width), F32),
            pltpu.VMEM((2, 8, width), F32),
            pltpu.VMEM((4, tall, width), F32),
            pltpu.VMEM((5, tall, width), F32),
            pltpu.VMEM((3, rows * own, width), BF16),
            pltpu.VMEM((batches, width, nobs), BF16),
            pltpu.VMEM((batches, nobs), jnp.int32),
            pltpu.VMEM((rows, width), BF16),
            pltpu.VMEM((n_piece, 2 * own, LANES), F32),
            pltpu.VMEM((n_slab, 2 * own, LANES), F32),
            pltpu.VMEM((2 * own, LANES), F32),
            pltpu.VMEM((members + own, LANES), F32),
            pltpu.VMEM((2 * batches, nobs), F32),
            pltpu.VMEM((batches - 1, nobs, batches * nobs), F32),
            pltpu.VMEM((batches, members, nobs), F32),
            pltpu.VMEM((batches, nobs, 3 * members), BF16),
            pltpu.VMEM((batches, 2 * members, nobs), BF16),
            pltpu.VMEM((batches, nobs, LANES), F32),
            pltpu.VMEM((batches, nobs, LANES), F32),
            pltpu.VMEM((rows, LANES), F32),
            pltpu.VMEM((members + own, batches * nobs), F32),
            dma((9,)),
            dma((4,)),
            dma((4,)),
            dma((n_slab,)),
            dma((n_slab,)),
            dma((n_mem,)),
            dma((n_mem,)),
            dma((n_piece,)),
            dma((n_piece,)),
            dma((chunks * n_mem,)),
            dma((chunks * n_mem,)),
        ],
        compiler_params=pltpu.CompilerParams(
            collective_id=0, has_side_effects=True, vmem_limit_bytes=60 << 20
        ),
    )(
        prior_concentrations,
        kappa,
        east_face_transport,
        v_north,
        land,
        obs_owner,
        obs_offset,
        obs_value,
        obs_var,
        jnp.swapaxes(obs_noise, 1, 2),
    )
    return out.reshape(members, rows, LANES)


def solution(mesh):
    placed = (
        P("mem", "slab", None),
        P("slab", None),
        P("slab", None),
        P("slab", None),
        P("slab", None),
        P(),
        P(),
        P(),
        P(),
        P(),
    )

    def whole(*arguments):
        prior, value = arguments[0], arguments[7]
        rows = prior.shape[1] // mesh.shape["slab"]
        geometry = geometry_of(mesh.shape, rows, *value.shape)
        return jax.shard_map(
            functools.partial(on_device, geometry),
            mesh=mesh,
            in_specs=placed,
            out_specs=P(None, "slab", "mem"),
            check_vma=False,
        )(*arguments)

    return whole
```

```python
import functools
import math

import jax
import jax.numpy as jnp
from jax import lax
from jax.experimental import pallas as pl
from jax.experimental.pallas import tpu as pltpu
from jax.sharding import PartitionSpec as P

F32 = jnp.float32
BF16 = jnp.bfloat16
PRECISE = lax.Precision.HIGHEST
MESH = pl.DeviceIdType.MESH
LANES = 128
OWN = 8
EARLY = 4
BASE = 8


def contract(a, b, dims):
    return lax.dot_general(
        a, b, ((dims[:1], dims[1:]), ((), ())), precision=PRECISE, preferred_element_type=F32
    )


def quick(a, b):
    return jnp.dot(a, b, preferred_element_type=F32)


def split(x):
    high = x.astype(BF16)
    return high, (x - high.astype(F32)).astype(BF16)


def solve_spd(system):
    rows, lanes = system.shape
    at = lax.broadcasted_iota(jnp.int32, (8, lanes), 0)

    def wide(x):
        return jnp.broadcast_to(x, (8, lanes))

    def block(_, parts):
        head, others = parts[0], parts[1:]
        columns = [wide(head[:, k : k + 1]) for k in range(8)]
        factors = [[wide(p[:, k : k + 1]) for k in range(8)] for p in others]
        for k in range(0, 8, 2):
            p, v = (wide(columns[k][r : r + 1]) for r in (k, k + 1))
            u, w = (wide(columns[k + 1][r : r + 1]) for r in (k, k + 1))
            inverse = 1.0 / (p * w - u * v)
            p, u, v, w = p * inverse, u * inverse, v * inverse, w * inverse

            def eliminate(x):
                upper, lower = wide(x[k : k + 1]), wide(x[k + 1 : k + 2])
                first = w * upper - u * lower
                second = p * lower - v * upper
                x = x - (columns[k] * first + columns[k + 1] * second)
                return jnp.where(at == k, first, jnp.where(at == k + 1, second, x))

            head = eliminate(head)
            for q in range(k + 2, 8):
                columns[q] = eliminate(columns[q])
        pivots = [wide(head[k : k + 1]) for k in range(8)]
        parts = []
        for p, f in zip(others, factors):
            terms = [f[k] * pivots[k] for k in range(8)]
            while len(terms) > 1:
                terms = [x + y for x, y in zip(terms[::2], terms[1::2])]
            parts.append(p - terms[0])
        return tuple(pltpu.roll(p, lanes - 8, 1) for p in parts + [head])

    parts = tuple(system[8 * i : 8 * i + 8] for i in range(rows // 8))
    parts = lax.fori_loop(0, rows // 8, block, parts)
    return jnp.concatenate(parts, 0)[:, :rows]


def kernel(
    geometry,
    prior_hbm,
    kappa_hbm,
    east_hbm,
    north_hbm,
    land_hbm,
    owner_ref,
    offset_hbm,
    value_hbm,
    var_hbm,
    noise_hbm,
    out_ref,
    prior_ref,
    kappa_ref,
    east_ref,
    north_ref,
    land_ref,
    offset_ref,
    value_ref,
    var_ref,
    noise_ref,
    padded,
    middle,
    forecast,
    states,
    stat_send,
    stat_recv,
    ext,
    coef,
    parts,
    column_of,
    line_of,
    sea,
    picked,
    reduce_buf,
    piece,
    gathered,
    sites,
    tapers,
    base_misfit,
    dcat,
    wcat,
    column_taper,
    row_site,
    wet_cols,
    site_cols,
    stage_sem,
    halo_send,
    halo_recv,
    reduce_send,
    reduce_recv,
    ring_send,
    ring_recv,
    share_send,
    share_recv,
    swap_send,
    swap_recv,
):
    n_slab, n_mem, n_piece, rb = geometry
    rows = kappa_ref.shape[0]
    width = kappa_ref.shape[1]
    members = OWN * n_mem
    batches, nobs = var_ref.shape
    total_obs = batches * nobs
    chunks = rows // rb
    extent = rows * n_slab // 2
    rate = 0.5 / (extent * extent)

    s = lax.axis_index("slab")
    z = lax.axis_index("mem")
    mine = lax.rem(s, n_piece)

    def slab_of(d):
        return lax.rem(s + d, n_slab)

    def mem_of(d):
        return lax.rem(z + d, n_mem)

    def piece_of(d):
        return s - mine + lax.rem(mine + d, n_piece)

    staged = [
        pltpu.make_async_copy(source, target, stage_sem.at[i])
        for i, (source, target) in enumerate(
            (
                (kappa_hbm, kappa_ref),
                (east_hbm, east_ref),
                (north_hbm, north_ref),
                (land_hbm, land_ref),
                (prior_hbm, prior_ref),
                (offset_hbm, offset_ref),
                (value_hbm, value_ref),
                (var_hbm, var_ref),
                (noise_hbm, noise_ref),
            )
        )
    ]
    for copy in staged:
        copy.start()

    barrier = pltpu.get_barrier_semaphore()
    for d in range(1, n_slab):
        pl.semaphore_signal(barrier, inc=1, device_id=(slab_of(d), z), device_id_type=MESH)
    for d in range(1, n_mem):
        pl.semaphore_signal(barrier, inc=1, device_id=(s, mem_of(d)), device_id_type=MESH)

    def fill(r):
        tile = prior_ref[:, pl.ds(r, 8), :]
        padded[pl.ds(r + 2, 8)] = jnp.swapaxes(tile, 0, 1)

    for copy in staged[:5]:
        copy.wait()
    wet = land_ref[...].astype(F32)
    ext[0, BASE : BASE + rows] = wet * kappa_ref[...]
    ext[1, BASE : BASE + rows] = wet
    ext[2, BASE : BASE + rows] = east_ref[...]
    ext[3, BASE : BASE + rows] = north_ref[...]
    for side, first in ((0, BASE), (1, BASE + rows - 2)):
        for field in range(4):
            stat_send[side, 2 * field : 2 * field + 2] = ext[field, first : first + 2]
    fill(0)
    fill(rows - 8)

    pl.semaphore_wait(barrier, n_slab - 1 + n_mem - 1)

    halo = []
    for side, (d, src, dst) in enumerate(
        ((n_slab - 1, 2, rows + 2), (1, rows, 0))
    ):
        target = (slab_of(d), z)
        halo.append(
            pltpu.make_async_remote_copy(
                src_ref=stat_send.at[side],
                dst_ref=stat_recv.at[side],
                send_sem=halo_send.at[2 * side],
                recv_sem=halo_recv.at[2 * side],
                device_id=target,
                device_id_type=MESH,
            )
        )
        halo.append(
            pltpu.make_async_remote_copy(
                src_ref=padded.at[pl.ds(src, 2)],
                dst_ref=padded.at[pl.ds(dst, 2)],
                send_sem=halo_send.at[2 * side + 1],
                recv_sem=halo_recv.at[2 * side + 1],
                device_id=target,
                device_id_type=MESH,
            )
        )
    for copy in halo:
        copy.start()

    def fill_rest(i, carry):
        fill(pl.multiple_of(8 * i, 8))
        return carry

    lax.fori_loop(1, rows // 8 - 1, fill_rest, 0)

    for copy in staged[5:]:
        copy.wait()
    offsets = offset_ref[...]
    batch_at = lax.broadcasted_iota(jnp.int32, offsets.shape, 0)
    owner_rows = jnp.zeros(offsets.shape, jnp.int32)
    for b in range(batches):
        owner_rows = jnp.where(batch_at == b, owner_ref[b] * rows, owner_rows)
    site_row = (owner_rows + offsets // width).astype(F32)
    site_col = (offsets % width).astype(F32)
    sites[0:batches] = site_row
    sites[batches : 2 * batches] = site_col
    line_of[...] = jnp.where(owner_rows == s * rows, offsets // width, -1)
    for b in range(batches):
        column = (offsets % width)[b : b + 1]
        for first in range(0, width, nobs):
            at = lax.broadcasted_iota(jnp.int32, (nobs, nobs), 0) + first
            column_of[b, first : first + nobs] = (at == column).astype(F32).astype(BF16)
    sea[...] = wet.astype(BF16)
    wet_cols[...] = land_ref[:, pl.ds(pl.multiple_of(z * LANES, LANES), LANES)].astype(F32)

    tall = ext.shape[1]
    lane = lax.broadcasted_iota(jnp.int32, (1, width), 1)
    not_last = (lane < width - 1).astype(F32)
    not_first = (lane > 0).astype(F32)

    def coefficients(first, count):
        conduct, open_, east, north = (ext[f, first : first + count + 2] for f in range(4))

        def leave_enter(near, near_open, far, far_open, flow):
            diffuse = jnp.sqrt(near * far)
            opened = near_open * far_open
            return (
                diffuse + opened * jnp.maximum(flow, 0.0),
                diffuse - opened * jnp.minimum(flow, 0.0),
            )

        mid = slice(1, count + 1)
        c, o = conduct[mid], open_[mid]
        c_next = pltpu.roll(c, width - 1, 1) * not_last
        o_next = pltpu.roll(o, width - 1, 1) * not_last
        out_e, in_e = leave_enter(c, o, c_next, o_next, east[mid])
        out_w = pltpu.roll(out_e, 1, 1) * not_first
        in_w = pltpu.roll(in_e, 1, 1) * not_first
        out_n, in_n = leave_enter(
            conduct[: count + 1], open_[: count + 1], conduct[1:], open_[1:], north[: count + 1]
        )
        where = slice(first + 1, first + 1 + count)
        coef[0, where] = o * (1.0 - out_e - in_w - out_n[1:] - in_n[:-1])
        coef[1, where] = o * in_e
        coef[2, where] = o * out_w
        coef[3, where] = o * in_n[1:]
        coef[4, where] = o * out_n[:-1]


    def stencil(source, at, row):
        def c(i):
            return jnp.broadcast_to(coef[i, pl.ds(row + BASE, 1), :], (OWN, width))

        here = source[at]
        return (
            c(0) * here
            + c(1) * pltpu.roll(here, width - 1, 1)
            + c(2) * pltpu.roll(here, 1, 1)
            + c(3) * source[at + 1]
            + c(4) * source[at - 1]
        )

    def first_step(i, carry):
        middle[i] = stencil(padded, i + 1, i - 1)
        return carry

    def second_step(i, carry):
        r = 2 * i
        pair = [stencil(middle, r + 1 + q, r + q) for q in range(2)]
        for q in range(2):
            forecast[r + q] = pair[q]
        value = jnp.concatenate(pair, 0)
        high = value.astype(BF16)
        rest = value - high.astype(F32)
        middle_part, low = split(rest)
        spot = pl.ds(pl.multiple_of(i * 2 * OWN, 2 * OWN), 2 * OWN)
        parts[0, spot] = high
        parts[1, spot] = middle_part
        parts[2, spot] = low
        return carry

    swaps = {}

    def advance(chunk):
        start = 0 if chunk == 0 else chunk * rb + (0 if chunk == 1 else 2)
        stop = rb if chunk == 0 else (chunk + 1) * rb + 2
        lax.fori_loop(start, stop, first_step, 0, unroll=8)
        lax.fori_loop(chunk * rb // 2, (chunk + 1) * rb // 2, second_step, 0, unroll=4)
        for d in range(1, n_mem):
            t = mem_of(d)
            swaps[chunk, d] = pltpu.make_async_remote_copy(
                src_ref=forecast.at[
                    pl.ds(chunk * rb, rb), :, pl.ds(pl.multiple_of(t * LANES, LANES), LANES)
                ],
                dst_ref=states.at[
                    pl.ds(chunk * rb, rb), pl.ds(pl.multiple_of(z * OWN, OWN), OWN), :
                ],
                send_sem=swap_send.at[chunk * n_mem + d],
                recv_sem=swap_recv.at[chunk * n_mem + d],
                device_id=(s, t),
                device_id_type=MESH,
            )

    order = [*range(1, chunks - 1), 0, chunks - 1]
    steps = [(chunk, d) for chunk in order for d in range(1, n_mem)]
    early = EARLY * (n_mem - 1) // 4
    for first in range(8, rows - 8, 8):
        coefficients(BASE - 1 + first, 8)
    for chunk in order:
        if chunk == 0:
            for copy in halo:
                copy.wait()

            low_ok = (s > 0).astype(F32)
            high_ok = (s < n_slab - 1).astype(F32)
            for field in range(4):
                ext[field, BASE - 2 : BASE] = stat_recv[1, 2 * field : 2 * field + 2] * low_ok
                ext[field, BASE + rows : BASE + rows + 2] = (
                    stat_recv[0, 2 * field : 2 * field + 2] * high_ok
                )
            for first in (0, rows - 8):
                coefficients(BASE - 1 + first, 8)
            coefficients(BASE - 2, 1)
            coefficients(BASE + rows - 1, 1)
        advance(chunk)
        for step in steps[:early]:
            if step[0] == chunk:
                swaps[step].start()
    states[:, pl.ds(pl.multiple_of(z * OWN, OWN), OWN), :] = forecast[
        :, :, pl.ds(pl.multiple_of(z * LANES, LANES), LANES)
    ]

    per_batch = nobs // LANES

    def reduce_to(t):
        return pltpu.make_async_remote_copy(
            src_ref=picked.at[lax.rem(t, n_piece)],
            dst_ref=reduce_buf.at[s],
            send_sem=reduce_send.at[t],
            recv_sem=reduce_recv.at[s],
            device_id=(t, z),
            device_id_type=MESH,
        )

    def reduce_from(t):
        return pltpu.make_async_remote_copy(
            src_ref=picked.at[mine],
            dst_ref=reduce_buf.at[t],
            send_sem=reduce_send.at[t],
            recv_sem=reduce_recv.at[t],
            device_id=(t, z),
            device_id_type=MESH,
        )

    def pick_batch(b, carry):
        line = line_of[pl.ds(b, 1), :]
        chosen_column = column_of[b]
        tracer = jnp.zeros((OWN, nobs), F32)
        at_line = lax.broadcasted_iota(jnp.int32, (rows, OWN, nobs), 0) == line[None]
        for part in range(3):
            part_here = quick(parts[part], chosen_column).reshape(rows, OWN, nobs)
            tracer = tracer + jnp.sum(jnp.where(at_line, part_here, 0.0), axis=0)
        sea_part = quick(sea[...], chosen_column)
        at_row = lax.broadcasted_iota(jnp.int32, (rows, nobs), 0)
        found = jnp.sum(jnp.where(line == at_row, sea_part, 0.0), axis=0, keepdims=True)
        for q in range(per_batch):
            lanes = slice(LANES * q, LANES * (q + 1))
            picked[b * per_batch + q, 0:OWN] = tracer[:, lanes]
            picked[b * per_batch + q, OWN : 2 * OWN] = jnp.broadcast_to(
                found[:, lanes], (OWN, LANES)
            )
            for group in range(0, n_slab, n_piece):
                t = group + b * per_batch + q

                @pl.when(t != s)
                def _():
                    reduce_to(t).start()

        return carry

    lax.fori_loop(0, batches, pick_batch, 0)

    flipped = sites[...].T
    for b in range(batches - 1):
        row_j = flipped[:, b : b + 1]
        col_j = flipped[:, batches + b : batches + b + 1]
        for later in range(b + 1, batches):
            g_row = row_j - sites[later : later + 1]
            g_col = col_j - sites[batches + later : batches + later + 1]
            tapers[b, :, nobs * later : nobs * (later + 1)] = jnp.exp(
                -rate * (g_row * g_row + g_col * g_col)
            )

    total = picked[mine]
    for d in range(1, n_slab):
        reduce_from(slab_of(d)).wait_recv()
        total = total + reduce_buf[slab_of(d)]
    piece[...] = total

    own_rows = pl.ds(pl.multiple_of(z * OWN, OWN), OWN)
    rings = []
    for d in range(1, n_mem):
        rings.append(
            pltpu.make_async_remote_copy(
                src_ref=piece.at[pl.ds(0, OWN)],
                dst_ref=gathered.at[own_rows],
                send_sem=ring_send.at[d],
                recv_sem=ring_recv.at[d],
                device_id=(s, mem_of(d)),
                device_id_type=MESH,
            )
        )
    for copy in rings:
        copy.start()
    gathered[own_rows] = total[0:OWN]
    gathered[members : members + OWN] = total[OWN : 2 * OWN]
    row0 = (s * rows).astype(F32)
    col0 = (z * LANES).astype(F32)
    columns = lax.broadcasted_iota(jnp.int32, (1, LANES), 1).astype(F32) + col0
    for b in range(batches):
        gap = flipped[:, batches + b : batches + b + 1] - columns
        column_taper[b] = jnp.exp(-rate * (gap * gap))
        row_site[b] = jnp.broadcast_to(flipped[:, b : b + 1], (nobs, LANES)) - row0
        base_misfit[b] = value_ref[b : b + 1] + jnp.sqrt(var_ref[b : b + 1]) * noise_ref[b]
    for copy in rings:
        copy.wait_recv()

    for step in steps[early:]:
        swaps[step].start()

    own_lanes = pl.ds(pl.multiple_of(mine * LANES, LANES), LANES)
    shares = []
    for d in range(1, n_piece):
        shares.append(
            pltpu.make_async_remote_copy(
                src_ref=gathered,
                dst_ref=site_cols.at[:, own_lanes],
                send_sem=share_send.at[d],
                recv_sem=share_recv.at[mine],
                device_id=(piece_of(d), z),
                device_id_type=MESH,
            )
        )
    for copy in shares:
        copy.start()
    site_cols[:, own_lanes] = gathered[...]

    def wait_pieces(which):
        for p in which:

            @pl.when(p != mine)
            def _():
                pltpu.make_async_remote_copy(
                    src_ref=gathered,
                    dst_ref=site_cols.at[:, pl.ds(p * LANES, LANES)],
                    send_sem=share_send.at[p],
                    recv_sem=share_recv.at[p],
                    device_id=(piece_of(1), z),
                    device_id_type=MESH,
                ).wait_recv()


    eye = (
        lax.broadcasted_iota(jnp.int32, (members, 2 * members), 0)
        == lax.broadcasted_iota(jnp.int32, (members, 2 * members), 1)
    ).astype(F32)
    wait_pieces(range(per_batch))
    for b in range(batches):
        now = slice(nobs * b, nobs * (b + 1))
        priors = site_cols[0:members, now]
        deviations = priors - jnp.mean(priors, axis=0, keepdims=True)
        inverse_var = 1.0 / var_ref[b : b + 1]
        misfit = base_misfit[b] - priors
        system = contract(
            deviations * inverse_var, jnp.concatenate([deviations, misfit], 0), (1, 1)
        ) + eye * (members - 1.0)
        high, low = split(deviations.T)
        dcat[b] = jnp.concatenate([high, high, low], 1)
        solved = solve_spd(system)
        if b == 0:
            wait_pieces(range(per_batch, n_piece))
        weights = (misfit - contract(solved, deviations, (0, 0))) * (
            inverse_var * (1.0 / (members - 1))
        )
        high, low = split(weights)
        wcat[b] = jnp.concatenate([high, low], 0)
        if b < batches - 1:
            rest = slice(nobs * (b + 1), total_obs)
            values = site_cols[0:members, rest]
            anomalies = values - jnp.mean(values, axis=0, keepdims=True)
            high, low = split(anomalies)
            covariance = quick(dcat[b], jnp.concatenate([high, low, high], 0))
            high, low = split(tapers[b, :, rest] * covariance)
            both = quick(wcat[b], high)
            change = both[:members] + both[members:] + quick(wcat[b, 0:members], low)
            site_cols[0:members, rest] = (
                values + change * site_cols[members : members + 1, rest]
            )

    for chunk in order:
        for d in range(1, n_mem):
            swaps[chunk, d].wait_recv()
        first = chunk * rb
        wet_here = jnp.concatenate(
            [wet_cols[first + q : first + q + 1] * math.exp(-rate * q * q) for q in range(rb)], 1
        )
        here = jnp.concatenate([states[first + q] for q in range(rb)], 1)

        def assimilate(b, here):
            anomalies = here - jnp.mean(here, axis=0, keepdims=True)
            high, low = split(anomalies)
            covariance = quick(dcat[b], jnp.concatenate([high, low, high], 0))
            gap = row_site[b] - float(first)
            step = jnp.exp((2.0 * rate) * gap)
            taper = jnp.exp(-rate * (gap * gap)) * column_taper[b]
            weighted = []
            for q in range(rb):
                weighted.append(covariance[:, LANES * q : LANES * (q + 1)] * taper)
                taper = taper * step
            high, low = split(jnp.concatenate(weighted, 1))
            both = quick(wcat[b], high)
            change = both[:members] + both[members:] + quick(wcat[b, 0:members], low)
            return here + change * wet_here

        here = lax.fori_loop(0, batches, assimilate, here)
        for q in range(rb):
            out_ref[pl.ds(first + q, members, stride=rows), :] = here[
                :, LANES * q : LANES * (q + 1)
            ]

    for d in range(1, n_slab):
        reduce_from(slab_of(d)).wait_send()
    for copy in [*swaps.values(), *rings, *shares]:
        copy.wait_send()


def geometry_of(mesh_shape, rows, batches, nobs):
    n_piece = batches * nobs // LANES
    return mesh_shape["slab"], mesh_shape["mem"], n_piece, rows // 4


def on_device(
    geometry,
    prior_concentrations,
    kappa,
    east_face_transport,
    v_north,
    land,
    obs_owner,
    obs_offset,
    obs_value,
    obs_var,
    obs_noise,
):
    n_slab, n_mem, n_piece, rb = geometry
    own, rows, width = prior_concentrations.shape
    batches, nobs = obs_value.shape
    members = own * n_mem
    chunks = rows // rb
    tall = rows + 2 * BASE
    vmem = pl.BlockSpec(memory_space=pltpu.VMEM)
    smem = pl.BlockSpec(memory_space=pltpu.SMEM)
    hbm = pl.BlockSpec(memory_space=pltpu.HBM)
    dma = pltpu.SemaphoreType.DMA
    out = pl.pallas_call(
        functools.partial(kernel, geometry),
        out_shape=jax.ShapeDtypeStruct((members * rows, LANES), F32),
        in_specs=[hbm] * 5 + [smem] + [hbm] * 4,
        out_specs=vmem,
        scratch_shapes=[
            pltpu.VMEM((own, rows, width), F32),
            pltpu.VMEM((rows, width), F32),
            pltpu.VMEM((rows, width), F32),
            pltpu.VMEM((rows, width), F32),
            pltpu.VMEM((rows, width), jnp.int32),
            pltpu.VMEM((batches, nobs), jnp.int32),
            pltpu.VMEM((batches, nobs), F32),
            pltpu.VMEM((batches, nobs), F32),
            pltpu.VMEM((batches, members, nobs), F32),
            pltpu.VMEM((rows + 4, own, width), F32),
            pltpu.VMEM((rows + 2, own, width), F32),
            pltpu.VMEM((rows, own, width), F32),
            pltpu.VMEM((rows, members, LANES), F32),
            pltpu.VMEM((2, 8, width), F32),
            pltpu.VMEM((2, 8, width), F32),
            pltpu.VMEM((4, tall, width), F32),
            pltpu.VMEM((5, tall, width), F32),
            pltpu.VMEM((3, rows * own, width), BF16),
            pltpu.VMEM((batches, width, nobs), BF16),
            pltpu.VMEM((batches, nobs), jnp.int32),
            pltpu.VMEM((rows, width), BF16),
            pltpu.VMEM((n_piece, 2 * own, LANES), F32),
            pltpu.VMEM((n_slab, 2 * own, LANES), F32),
            pltpu.VMEM((2 * own, LANES), F32),
            pltpu.VMEM((members + own, LANES), F32),
            pltpu.VMEM((2 * batches, nobs), F32),
            pltpu.VMEM((batches - 1, nobs, batches * nobs), F32),
            pltpu.VMEM((batches, members, nobs), F32),
            pltpu.VMEM((batches, nobs, 3 * members), BF16),
            pltpu.VMEM((batches, 2 * members, nobs), BF16),
            pltpu.VMEM((batches, nobs, LANES), F32),
            pltpu.VMEM((batches, nobs, LANES), F32),
            pltpu.VMEM((rows, LANES), F32),
            pltpu.VMEM((members + own, batches * nobs), F32),
            dma((9,)),
            dma((4,)),
            dma((4,)),
            dma((n_slab,)),
            dma((n_slab,)),
            dma((n_mem,)),
            dma((n_mem,)),
            dma((n_piece,)),
            dma((n_piece,)),
            dma((chunks * n_mem,)),
            dma((chunks * n_mem,)),
        ],
        compiler_params=pltpu.CompilerParams(
            collective_id=0, has_side_effects=True, vmem_limit_bytes=60 << 20
        ),
    )(
        prior_concentrations,
        kappa,
        east_face_transport,
        v_north,
        land,
        obs_owner,
        obs_offset,
        obs_value,
        obs_var,
        jnp.swapaxes(obs_noise, 1, 2),
    )
    return out.reshape(members, rows, LANES)


def solution(mesh):
    placed = (
        P("mem", "slab", None),
        P("slab", None),
        P("slab", None),
        P("slab", None),
        P("slab", None),
        P(),
        P(),
        P(),
        P(),
        P(),
    )

    def whole(*arguments):
        prior, value = arguments[0], arguments[7]
        rows = prior.shape[1] // mesh.shape["slab"]
        geometry = geometry_of(mesh.shape, rows, *value.shape)
        return jax.shard_map(
            functools.partial(on_device, geometry),
            mesh=mesh,
            in_specs=placed,
            out_specs=P(None, "slab", "mem"),
            check_vma=False,
        )(*arguments)

    return whole
```

```python
import functools
import math

import jax
import jax.numpy as jnp
from jax import lax
from jax.experimental import pallas as pl
from jax.experimental.pallas import tpu as pltpu
from jax.sharding import PartitionSpec as P

F32 = jnp.float32
BF16 = jnp.bfloat16
PRECISE = lax.Precision.HIGHEST
MESH = pl.DeviceIdType.MESH
LANES = 128
OWN = 8
EARLY = 5
BASE = 8


def contract(a, b, dims):
    return lax.dot_general(
        a, b, ((dims[:1], dims[1:]), ((), ())), precision=PRECISE, preferred_element_type=F32
    )


def quick(a, b):
    return jnp.dot(a, b, preferred_element_type=F32)


def split(x):
    high = x.astype(BF16)
    return high, (x - high.astype(F32)).astype(BF16)


def solve_spd(system):
    rows, lanes = system.shape
    at = lax.broadcasted_iota(jnp.int32, (8, lanes), 0)

    def wide(x):
        return jnp.broadcast_to(x, (8, lanes))

    def block(_, parts):
        head, others = parts[0], parts[1:]
        columns = [wide(head[:, k : k + 1]) for k in range(8)]
        factors = [[wide(p[:, k : k + 1]) for k in range(8)] for p in others]
        for k in range(0, 8, 2):
            p, v = (wide(columns[k][r : r + 1]) for r in (k, k + 1))
            u, w = (wide(columns[k + 1][r : r + 1]) for r in (k, k + 1))
            inverse = 1.0 / (p * w - u * v)
            p, u, v, w = p * inverse, u * inverse, v * inverse, w * inverse

            def eliminate(x):
                upper, lower = wide(x[k : k + 1]), wide(x[k + 1 : k + 2])
                first = w * upper - u * lower
                second = p * lower - v * upper
                x = x - (columns[k] * first + columns[k + 1] * second)
                return jnp.where(at == k, first, jnp.where(at == k + 1, second, x))

            head = eliminate(head)
            for q in range(k + 2, 8):
                columns[q] = eliminate(columns[q])
        pivots = [wide(head[k : k + 1]) for k in range(8)]
        parts = []
        for p, f in zip(others, factors):
            terms = [f[k] * pivots[k] for k in range(8)]
            while len(terms) > 1:
                terms = [x + y for x, y in zip(terms[::2], terms[1::2])]
            parts.append(p - terms[0])
        return tuple(pltpu.roll(p, lanes - 8, 1) for p in parts + [head])

    parts = tuple(system[8 * i : 8 * i + 8] for i in range(rows // 8))
    parts = lax.fori_loop(0, rows // 8, block, parts)
    return jnp.concatenate(parts, 0)[:, :rows]


def kernel(
    geometry,
    prior_hbm,
    kappa_hbm,
    east_hbm,
    north_hbm,
    land_hbm,
    owner_ref,
    offset_hbm,
    value_hbm,
    var_hbm,
    noise_hbm,
    out_ref,
    prior_ref,
    kappa_ref,
    east_ref,
    north_ref,
    land_ref,
    offset_ref,
    value_ref,
    var_ref,
    noise_ref,
    padded,
    middle,
    forecast,
    states,
    stat_send,
    stat_recv,
    ext,
    coef,
    parts,
    column_of,
    line_of,
    sea,
    picked,
    reduce_buf,
    piece,
    gathered,
    sites,
    tapers,
    base_misfit,
    dcat,
    wcat,
    column_taper,
    row_site,
    wet_cols,
    site_cols,
    stage_sem,
    halo_send,
    halo_recv,
    reduce_send,
    reduce_recv,
    ring_send,
    ring_recv,
    share_send,
    share_recv,
    swap_send,
    swap_recv,
):
    n_slab, n_mem, n_piece, rb = geometry
    rows = kappa_ref.shape[0]
    width = kappa_ref.shape[1]
    members = OWN * n_mem
    batches, nobs = var_ref.shape
    total_obs = batches * nobs
    chunks = rows // rb
    extent = rows * n_slab // 2
    rate = 0.5 / (extent * extent)

    s = lax.axis_index("slab")
    z = lax.axis_index("mem")
    mine = lax.rem(s, n_piece)

    def slab_of(d):
        return lax.rem(s + d, n_slab)

    def mem_of(d):
        return lax.rem(z + d, n_mem)

    def piece_of(d):
        return s - mine + lax.rem(mine + d, n_piece)

    staged = [
        pltpu.make_async_copy(source, target, stage_sem.at[i])
        for i, (source, target) in enumerate(
            (
                (kappa_hbm, kappa_ref),
                (east_hbm, east_ref),
                (north_hbm, north_ref),
                (land_hbm, land_ref),
                (prior_hbm, prior_ref),
                (offset_hbm, offset_ref),
                (value_hbm, value_ref),
                (var_hbm, var_ref),
                (noise_hbm, noise_ref),
            )
        )
    ]
    for copy in staged:
        copy.start()

    barrier = pltpu.get_barrier_semaphore()
    for d in range(1, n_slab):
        pl.semaphore_signal(barrier, inc=1, device_id=(slab_of(d), z), device_id_type=MESH)
    for d in range(1, n_mem):
        pl.semaphore_signal(barrier, inc=1, device_id=(s, mem_of(d)), device_id_type=MESH)

    def fill(r):
        tile = prior_ref[:, pl.ds(r, 8), :]
        padded[pl.ds(r + 2, 8)] = jnp.swapaxes(tile, 0, 1)

    for copy in staged[:5]:
        copy.wait()
    wet = land_ref[...].astype(F32)
    ext[0, BASE : BASE + rows] = wet * kappa_ref[...]
    ext[1, BASE : BASE + rows] = wet
    ext[2, BASE : BASE + rows] = east_ref[...]
    ext[3, BASE : BASE + rows] = north_ref[...]
    for side, first in ((0, BASE), (1, BASE + rows - 2)):
        for field in range(4):
            stat_send[side, 2 * field : 2 * field + 2] = ext[field, first : first + 2]
    fill(0)
    fill(rows - 8)

    pl.semaphore_wait(barrier, n_slab - 1 + n_mem - 1)

    halo = []
    for side, (d, src, dst) in enumerate(
        ((n_slab - 1, 2, rows + 2), (1, rows, 0))
    ):
        target = (slab_of(d), z)
        halo.append(
            pltpu.make_async_remote_copy(
                src_ref=stat_send.at[side],
                dst_ref=stat_recv.at[side],
                send_sem=halo_send.at[2 * side],
                recv_sem=halo_recv.at[2 * side],
                device_id=target,
                device_id_type=MESH,
            )
        )
        halo.append(
            pltpu.make_async_remote_copy(
                src_ref=padded.at[pl.ds(src, 2)],
                dst_ref=padded.at[pl.ds(dst, 2)],
                send_sem=halo_send.at[2 * side + 1],
                recv_sem=halo_recv.at[2 * side + 1],
                device_id=target,
                device_id_type=MESH,
            )
        )
    for copy in halo:
        copy.start()

    def fill_rest(i, carry):
        fill(pl.multiple_of(8 * i, 8))
        return carry

    lax.fori_loop(1, rows // 8 - 1, fill_rest, 0)

    for copy in staged[5:]:
        copy.wait()
    offsets = offset_ref[...]
    batch_at = lax.broadcasted_iota(jnp.int32, offsets.shape, 0)
    owner_rows = jnp.zeros(offsets.shape, jnp.int32)
    for b in range(batches):
        owner_rows = jnp.where(batch_at == b, owner_ref[b] * rows, owner_rows)
    site_row = (owner_rows + offsets // width).astype(F32)
    site_col = (offsets % width).astype(F32)
    sites[0:batches] = site_row
    sites[batches : 2 * batches] = site_col
    line_of[...] = jnp.where(owner_rows == s * rows, offsets // width, -1)
    for b in range(batches):
        column = (offsets % width)[b : b + 1]
        for first in range(0, width, nobs):
            at = lax.broadcasted_iota(jnp.int32, (nobs, nobs), 0) + first
            column_of[b, first : first + nobs] = (at == column).astype(F32).astype(BF16)
    sea[...] = wet.astype(BF16)
    wet_cols[...] = land_ref[:, pl.ds(pl.multiple_of(z * LANES, LANES), LANES)].astype(F32)

    tall = ext.shape[1]
    lane = lax.broadcasted_iota(jnp.int32, (1, width), 1)
    not_last = (lane < width - 1).astype(F32)
    not_first = (lane > 0).astype(F32)

    def coefficients(first, count):
        conduct, open_, east, north = (ext[f, first : first + count + 2] for f in range(4))

        def leave_enter(near, near_open, far, far_open, flow):
            diffuse = jnp.sqrt(near * far)
            opened = near_open * far_open
            return (
                diffuse + opened * jnp.maximum(flow, 0.0),
                diffuse - opened * jnp.minimum(flow, 0.0),
            )

        mid = slice(1, count + 1)
        c, o = conduct[mid], open_[mid]
        c_next = pltpu.roll(c, width - 1, 1) * not_last
        o_next = pltpu.roll(o, width - 1, 1) * not_last
        out_e, in_e = leave_enter(c, o, c_next, o_next, east[mid])
        out_w = pltpu.roll(out_e, 1, 1) * not_first
        in_w = pltpu.roll(in_e, 1, 1) * not_first
        out_n, in_n = leave_enter(
            conduct[: count + 1], open_[: count + 1], conduct[1:], open_[1:], north[: count + 1]
        )
        where = slice(first + 1, first + 1 + count)
        coef[0, where] = o * (1.0 - out_e - in_w - out_n[1:] - in_n[:-1])
        coef[1, where] = o * in_e
        coef[2, where] = o * out_w
        coef[3, where] = o * in_n[1:]
        coef[4, where] = o * out_n[:-1]


    def stencil(source, at, row):
        def c(i):
            return jnp.broadcast_to(coef[i, pl.ds(row + BASE, 1), :], (OWN, width))

        here = source[at]
        return (
            c(0) * here
            + c(1) * pltpu.roll(here, width - 1, 1)
            + c(2) * pltpu.roll(here, 1, 1)
            + c(3) * source[at + 1]
            + c(4) * source[at - 1]
        )

    def first_step(i, carry):
        middle[i] = stencil(padded, i + 1, i - 1)
        return carry

    def second_step(i, carry):
        r = 2 * i
        pair = [stencil(middle, r + 1 + q, r + q) for q in range(2)]
        for q in range(2):
            forecast[r + q] = pair[q]
        value = jnp.concatenate(pair, 0)
        high = value.astype(BF16)
        rest = value - high.astype(F32)
        middle_part, low = split(rest)
        spot = pl.ds(pl.multiple_of(i * 2 * OWN, 2 * OWN), 2 * OWN)
        parts[0, spot] = high
        parts[1, spot] = middle_part
        parts[2, spot] = low
        return carry

    swaps = {}

    def advance(chunk):
        start = 0 if chunk == 0 else chunk * rb + (0 if chunk == 1 else 2)
        stop = rb if chunk == 0 else (chunk + 1) * rb + 2
        lax.fori_loop(start, stop, first_step, 0, unroll=8)
        lax.fori_loop(chunk * rb // 2, (chunk + 1) * rb // 2, second_step, 0, unroll=4)
        for d in range(1, n_mem):
            t = mem_of(d)
            swaps[chunk, d] = pltpu.make_async_remote_copy(
                src_ref=forecast.at[
                    pl.ds(chunk * rb, rb), :, pl.ds(pl.multiple_of(t * LANES, LANES), LANES)
                ],
                dst_ref=states.at[
                    pl.ds(chunk * rb, rb), pl.ds(pl.multiple_of(z * OWN, OWN), OWN), :
                ],
                send_sem=swap_send.at[chunk * n_mem + d],
                recv_sem=swap_recv.at[chunk * n_mem + d],
                device_id=(s, t),
                device_id_type=MESH,
            )

    order = [*range(1, chunks - 1), 0, chunks - 1]
    steps = [(chunk, d) for chunk in order for d in range(1, n_mem)]
    early = EARLY * (n_mem - 1) // 4
    for first in range(8, rows - 8, 8):
        coefficients(BASE - 1 + first, 8)
    for chunk in order:
        if chunk == 0:
            for copy in halo:
                copy.wait()

            low_ok = (s > 0).astype(F32)
            high_ok = (s < n_slab - 1).astype(F32)
            for field in range(4):
                ext[field, BASE - 2 : BASE] = stat_recv[1, 2 * field : 2 * field + 2] * low_ok
                ext[field, BASE + rows : BASE + rows + 2] = (
                    stat_recv[0, 2 * field : 2 * field + 2] * high_ok
                )
            for first in (0, rows - 8):
                coefficients(BASE - 1 + first, 8)
            coefficients(BASE - 2, 1)
            coefficients(BASE + rows - 1, 1)
        advance(chunk)
        for step in steps[:early]:
            if step[0] == chunk:
                swaps[step].start()
    states[:, pl.ds(pl.multiple_of(z * OWN, OWN), OWN), :] = forecast[
        :, :, pl.ds(pl.multiple_of(z * LANES, LANES), LANES)
    ]

    per_batch = nobs // LANES

    def reduce_to(t):
        return pltpu.make_async_remote_copy(
            src_ref=picked.at[lax.rem(t, n_piece)],
            dst_ref=reduce_buf.at[s],
            send_sem=reduce_send.at[t],
            recv_sem=reduce_recv.at[s],
            device_id=(t, z),
            device_id_type=MESH,
        )

    def reduce_from(t):
        return pltpu.make_async_remote_copy(
            src_ref=picked.at[mine],
            dst_ref=reduce_buf.at[t],
            send_sem=reduce_send.at[t],
            recv_sem=reduce_recv.at[t],
            device_id=(t, z),
            device_id_type=MESH,
        )

    def pick_batch(b, carry):
        line = line_of[pl.ds(b, 1), :]
        chosen_column = column_of[b]
        tracer = jnp.zeros((OWN, nobs), F32)
        at_line = lax.broadcasted_iota(jnp.int32, (rows, OWN, nobs), 0) == line[None]
        for part in range(3):
            part_here = quick(parts[part], chosen_column).reshape(rows, OWN, nobs)
            tracer = tracer + jnp.sum(jnp.where(at_line, part_here, 0.0), axis=0)
        sea_part = quick(sea[...], chosen_column)
        at_row = lax.broadcasted_iota(jnp.int32, (rows, nobs), 0)
        found = jnp.sum(jnp.where(line == at_row, sea_part, 0.0), axis=0, keepdims=True)
        for q in range(per_batch):
            lanes = slice(LANES * q, LANES * (q + 1))
            picked[b * per_batch + q, 0:OWN] = tracer[:, lanes]
            picked[b * per_batch + q, OWN : 2 * OWN] = jnp.broadcast_to(
                found[:, lanes], (OWN, LANES)
            )
            for group in range(0, n_slab, n_piece):
                t = group + b * per_batch + q

                @pl.when(t != s)
                def _():
                    reduce_to(t).start()

        return carry

    lax.fori_loop(0, batches, pick_batch, 0)

    flipped = sites[...].T
    for b in range(batches - 1):
        row_j = flipped[:, b : b + 1]
        col_j = flipped[:, batches + b : batches + b + 1]
        for later in range(b + 1, batches):
            g_row = row_j - sites[later : later + 1]
            g_col = col_j - sites[batches + later : batches + later + 1]
            tapers[b, :, nobs * later : nobs * (later + 1)] = jnp.exp(
                -rate * (g_row * g_row + g_col * g_col)
            )

    total = picked[mine]
    for d in range(1, n_slab):
        reduce_from(slab_of(d)).wait_recv()
        total = total + reduce_buf[slab_of(d)]
    piece[...] = total

    own_rows = pl.ds(pl.multiple_of(z * OWN, OWN), OWN)
    rings = []
    for d in range(1, n_mem):
        rings.append(
            pltpu.make_async_remote_copy(
                src_ref=piece.at[pl.ds(0, OWN)],
                dst_ref=gathered.at[own_rows],
                send_sem=ring_send.at[d],
                recv_sem=ring_recv.at[d],
                device_id=(s, mem_of(d)),
                device_id_type=MESH,
            )
        )
    for copy in rings:
        copy.start()
    gathered[own_rows] = total[0:OWN]
    gathered[members : members + OWN] = total[OWN : 2 * OWN]
    row0 = (s * rows).astype(F32)
    col0 = (z * LANES).astype(F32)
    columns = lax.broadcasted_iota(jnp.int32, (1, LANES), 1).astype(F32) + col0
    for b in range(batches):
        gap = flipped[:, batches + b : batches + b + 1] - columns
        column_taper[b] = jnp.exp(-rate * (gap * gap))
        row_site[b] = jnp.broadcast_to(flipped[:, b : b + 1], (nobs, LANES)) - row0
        base_misfit[b] = value_ref[b : b + 1] + jnp.sqrt(var_ref[b : b + 1]) * noise_ref[b]
    for copy in rings:
        copy.wait_recv()


    own_lanes = pl.ds(pl.multiple_of(mine * LANES, LANES), LANES)
    shares = []
    for d in range(1, n_piece):
        shares.append(
            pltpu.make_async_remote_copy(
                src_ref=gathered,
                dst_ref=site_cols.at[:, own_lanes],
                send_sem=share_send.at[d],
                recv_sem=share_recv.at[mine],
                device_id=(piece_of(d), z),
                device_id_type=MESH,
            )
        )
    for copy in shares:
        copy.start()
    for step in steps[early:]:
        swaps[step].start()
    site_cols[:, own_lanes] = gathered[...]

    def wait_pieces(which):
        for p in which:

            @pl.when(p != mine)
            def _():
                pltpu.make_async_remote_copy(
                    src_ref=gathered,
                    dst_ref=site_cols.at[:, pl.ds(p * LANES, LANES)],
                    send_sem=share_send.at[p],
                    recv_sem=share_recv.at[p],
                    device_id=(piece_of(1), z),
                    device_id_type=MESH,
                ).wait_recv()


    eye = (
        lax.broadcasted_iota(jnp.int32, (members, 2 * members), 0)
        == lax.broadcasted_iota(jnp.int32, (members, 2 * members), 1)
    ).astype(F32)
    wait_pieces(range(per_batch))
    for b in range(batches):
        now = slice(nobs * b, nobs * (b + 1))
        priors = site_cols[0:members, now]
        deviations = priors - jnp.mean(priors, axis=0, keepdims=True)
        inverse_var = 1.0 / var_ref[b : b + 1]
        misfit = base_misfit[b] - priors
        system = contract(
            deviations * inverse_var, jnp.concatenate([deviations, misfit], 0), (1, 1)
        ) + eye * (members - 1.0)
        high, low = split(deviations.T)
        dcat[b] = jnp.concatenate([high, high, low], 1)
        solved = solve_spd(system)
        if b == 0:
            wait_pieces(range(per_batch, n_piece))
        weights = (misfit - contract(solved, deviations, (0, 0))) * (
            inverse_var * (1.0 / (members - 1))
        )
        high, low = split(weights)
        wcat[b] = jnp.concatenate([high, low], 0)
        if b < batches - 1:
            rest = slice(nobs * (b + 1), total_obs)
            values = site_cols[0:members, rest]
            anomalies = values - jnp.mean(values, axis=0, keepdims=True)
            high, low = split(anomalies)
            covariance = quick(dcat[b], jnp.concatenate([high, low, high], 0))
            high, low = split(tapers[b, :, rest] * covariance)
            both = quick(wcat[b], high)
            change = both[:members] + both[members:] + quick(wcat[b, 0:members], low)
            site_cols[0:members, rest] = (
                values + change * site_cols[members : members + 1, rest]
            )

    for chunk in order:
        for d in range(1, n_mem):
            swaps[chunk, d].wait_recv()
        first = chunk * rb
        wet_here = jnp.concatenate(
            [wet_cols[first + q : first + q + 1] * math.exp(-rate * q * q) for q in range(rb)], 1
        )
        here = jnp.concatenate([states[first + q] for q in range(rb)], 1)

        def assimilate(b, here):
            anomalies = here - jnp.mean(here, axis=0, keepdims=True)
            high, low = split(anomalies)
            covariance = quick(dcat[b], jnp.concatenate([high, low, high], 0))
            gap = row_site[b] - float(first)
            step = jnp.exp((2.0 * rate) * gap)
            taper = jnp.exp(-rate * (gap * gap)) * column_taper[b]
            weighted = []
            for q in range(rb):
                weighted.append(covariance[:, LANES * q : LANES * (q + 1)] * taper)
                taper = taper * step
            high, low = split(jnp.concatenate(weighted, 1))
            both = quick(wcat[b], high)
            change = both[:members] + both[members:] + quick(wcat[b, 0:members], low)
            return here + change * wet_here

        here = lax.fori_loop(0, batches, assimilate, here)
        for q in range(rb):
            out_ref[pl.ds(first + q, members, stride=rows), :] = here[
                :, LANES * q : LANES * (q + 1)
            ]

    for d in range(1, n_slab):
        reduce_from(slab_of(d)).wait_send()
    for copy in [*swaps.values(), *rings, *shares]:
        copy.wait_send()


def geometry_of(mesh_shape, rows, batches, nobs):
    n_piece = batches * nobs // LANES
    return mesh_shape["slab"], mesh_shape["mem"], n_piece, rows // 4


def on_device(
    geometry,
    prior_concentrations,
    kappa,
    east_face_transport,
    v_north,
    land,
    obs_owner,
    obs_offset,
    obs_value,
    obs_var,
    obs_noise,
):
    n_slab, n_mem, n_piece, rb = geometry
    own, rows, width = prior_concentrations.shape
    batches, nobs = obs_value.shape
    members = own * n_mem
    chunks = rows // rb
    tall = rows + 2 * BASE
    vmem = pl.BlockSpec(memory_space=pltpu.VMEM)
    smem = pl.BlockSpec(memory_space=pltpu.SMEM)
    hbm = pl.BlockSpec(memory_space=pltpu.HBM)
    dma = pltpu.SemaphoreType.DMA
    out = pl.pallas_call(
        functools.partial(kernel, geometry),
        out_shape=jax.ShapeDtypeStruct((members * rows, LANES), F32),
        in_specs=[hbm] * 5 + [smem] + [hbm] * 4,
        out_specs=vmem,
        scratch_shapes=[
            pltpu.VMEM((own, rows, width), F32),
            pltpu.VMEM((rows, width), F32),
            pltpu.VMEM((rows, width), F32),
            pltpu.VMEM((rows, width), F32),
            pltpu.VMEM((rows, width), jnp.int32),
            pltpu.VMEM((batches, nobs), jnp.int32),
            pltpu.VMEM((batches, nobs), F32),
            pltpu.VMEM((batches, nobs), F32),
            pltpu.VMEM((batches, members, nobs), F32),
            pltpu.VMEM((rows + 4, own, width), F32),
            pltpu.VMEM((rows + 2, own, width), F32),
            pltpu.VMEM((rows, own, width), F32),
            pltpu.VMEM((rows, members, LANES), F32),
            pltpu.VMEM((2, 8, width), F32),
            pltpu.VMEM((2, 8, width), F32),
            pltpu.VMEM((4, tall, width), F32),
            pltpu.VMEM((5, tall, width), F32),
            pltpu.VMEM((3, rows * own, width), BF16),
            pltpu.VMEM((batches, width, nobs), BF16),
            pltpu.VMEM((batches, nobs), jnp.int32),
            pltpu.VMEM((rows, width), BF16),
            pltpu.VMEM((n_piece, 2 * own, LANES), F32),
            pltpu.VMEM((n_slab, 2 * own, LANES), F32),
            pltpu.VMEM((2 * own, LANES), F32),
            pltpu.VMEM((members + own, LANES), F32),
            pltpu.VMEM((2 * batches, nobs), F32),
            pltpu.VMEM((batches - 1, nobs, batches * nobs), F32),
            pltpu.VMEM((batches, members, nobs), F32),
            pltpu.VMEM((batches, nobs, 3 * members), BF16),
            pltpu.VMEM((batches, 2 * members, nobs), BF16),
            pltpu.VMEM((batches, nobs, LANES), F32),
            pltpu.VMEM((batches, nobs, LANES), F32),
            pltpu.VMEM((rows, LANES), F32),
            pltpu.VMEM((members + own, batches * nobs), F32),
            dma((9,)),
            dma((4,)),
            dma((4,)),
            dma((n_slab,)),
            dma((n_slab,)),
            dma((n_mem,)),
            dma((n_mem,)),
            dma((n_piece,)),
            dma((n_piece,)),
            dma((chunks * n_mem,)),
            dma((chunks * n_mem,)),
        ],
        compiler_params=pltpu.CompilerParams(
            collective_id=0, has_side_effects=True, vmem_limit_bytes=60 << 20
        ),
    )(
        prior_concentrations,
        kappa,
        east_face_transport,
        v_north,
        land,
        obs_owner,
        obs_offset,
        obs_value,
        obs_var,
        jnp.swapaxes(obs_noise, 1, 2),
    )
    return out.reshape(members, rows, LANES)


def solution(mesh):
    placed = (
        P("mem", "slab", None),
        P("slab", None),
        P("slab", None),
        P("slab", None),
        P("slab", None),
        P(),
        P(),
        P(),
        P(),
        P(),
    )

    def whole(*arguments):
        prior, value = arguments[0], arguments[7]
        rows = prior.shape[1] // mesh.shape["slab"]
        geometry = geometry_of(mesh.shape, rows, *value.shape)
        return jax.shard_map(
            functools.partial(on_device, geometry),
            mesh=mesh,
            in_specs=placed,
            out_specs=P(None, "slab", "mem"),
            check_vma=False,
        )(*arguments)

    return whole
```

```python
import functools
import math

import jax
import jax.numpy as jnp
from jax import lax
from jax.experimental import pallas as pl
from jax.experimental.pallas import tpu as pltpu
from jax.sharding import PartitionSpec as P

F32 = jnp.float32
BF16 = jnp.bfloat16
PRECISE = lax.Precision.HIGHEST
MESH = pl.DeviceIdType.MESH
LANES = 128
OWN = 8
EARLY = 5
BASE = 8


def contract(a, b, dims):
    return lax.dot_general(
        a, b, ((dims[:1], dims[1:]), ((), ())), precision=PRECISE, preferred_element_type=F32
    )


def quick(a, b):
    return jnp.dot(a, b, preferred_element_type=F32)


def split(x):
    high = x.astype(BF16)
    return high, (x - high.astype(F32)).astype(BF16)


def solve_spd(system):
    rows, lanes = system.shape
    at = lax.broadcasted_iota(jnp.int32, (8, lanes), 0)

    def wide(x):
        return jnp.broadcast_to(x, (8, lanes))

    def block(_, parts):
        head, others = parts[0], parts[1:]
        columns = [wide(head[:, k : k + 1]) for k in range(8)]
        factors = [[wide(p[:, k : k + 1]) for k in range(8)] for p in others]
        for k in range(0, 8, 2):
            p, v = (wide(columns[k][r : r + 1]) for r in (k, k + 1))
            u, w = (wide(columns[k + 1][r : r + 1]) for r in (k, k + 1))
            inverse = 1.0 / (p * w - u * v)
            p, u, v, w = p * inverse, u * inverse, v * inverse, w * inverse

            def eliminate(x):
                upper, lower = wide(x[k : k + 1]), wide(x[k + 1 : k + 2])
                first = w * upper - u * lower
                second = p * lower - v * upper
                x = x - (columns[k] * first + columns[k + 1] * second)
                return jnp.where(at == k, first, jnp.where(at == k + 1, second, x))

            head = eliminate(head)
            for q in range(k + 2, 8):
                columns[q] = eliminate(columns[q])
        pivots = [wide(head[k : k + 1]) for k in range(8)]
        parts = []
        for p, f in zip(others, factors):
            terms = [f[k] * pivots[k] for k in range(8)]
            while len(terms) > 1:
                terms = [x + y for x, y in zip(terms[::2], terms[1::2])]
            parts.append(p - terms[0])
        return tuple(pltpu.roll(p, lanes - 8, 1) for p in parts + [head])

    parts = tuple(system[8 * i : 8 * i + 8] for i in range(rows // 8))
    parts = lax.fori_loop(0, rows // 8, block, parts)
    return jnp.concatenate(parts, 0)[:, :rows]


def kernel(
    geometry,
    prior_hbm,
    kappa_hbm,
    east_hbm,
    north_hbm,
    land_hbm,
    owner_ref,
    offset_hbm,
    value_hbm,
    var_hbm,
    noise_hbm,
    out_ref,
    prior_ref,
    kappa_ref,
    east_ref,
    north_ref,
    land_ref,
    offset_ref,
    value_ref,
    var_ref,
    noise_ref,
    padded,
    middle,
    forecast,
    states,
    stat_send,
    stat_recv,
    ext,
    coef,
    parts,
    column_of,
    line_of,
    sea,
    picked,
    reduce_buf,
    piece,
    gathered,
    sites,
    tapers,
    base_misfit,
    dcat,
    wcat,
    column_taper,
    row_site,
    wet_cols,
    site_cols,
    stage_sem,
    halo_send,
    halo_recv,
    reduce_send,
    reduce_recv,
    ring_send,
    ring_recv,
    share_send,
    share_recv,
    swap_send,
    swap_recv,
):
    n_slab, n_mem, n_piece, rb = geometry
    rows = kappa_ref.shape[0]
    width = kappa_ref.shape[1]
    members = OWN * n_mem
    batches, nobs = var_ref.shape
    total_obs = batches * nobs
    chunks = rows // rb
    extent = rows * n_slab // 2
    rate = 0.5 / (extent * extent)

    s = lax.axis_index("slab")
    z = lax.axis_index("mem")
    mine = lax.rem(s, n_piece)

    def slab_of(d):
        return lax.rem(s + d, n_slab)

    def mem_of(d):
        return lax.rem(z + d, n_mem)

    def piece_of(d):
        return s - mine + lax.rem(mine + d, n_piece)

    staged = [
        pltpu.make_async_copy(source, target, stage_sem.at[i])
        for i, (source, target) in enumerate(
            (
                (kappa_hbm, kappa_ref),
                (east_hbm, east_ref),
                (north_hbm, north_ref),
                (land_hbm, land_ref),
                (prior_hbm, prior_ref),
                (offset_hbm, offset_ref),
                (value_hbm, value_ref),
                (var_hbm, var_ref),
                (noise_hbm, noise_ref),
            )
        )
    ]
    for copy in staged:
        copy.start()

    barrier = pltpu.get_barrier_semaphore()
    for d in range(1, n_slab):
        pl.semaphore_signal(barrier, inc=1, device_id=(slab_of(d), z), device_id_type=MESH)
    for d in range(1, n_mem):
        pl.semaphore_signal(barrier, inc=1, device_id=(s, mem_of(d)), device_id_type=MESH)

    def fill(r):
        tile = prior_ref[:, pl.ds(r, 8), :]
        padded[pl.ds(r + 2, 8)] = jnp.swapaxes(tile, 0, 1)

    for copy in staged[:5]:
        copy.wait()
    wet = land_ref[...].astype(F32)
    ext[0, BASE : BASE + rows] = wet * kappa_ref[...]
    ext[1, BASE : BASE + rows] = wet
    ext[2, BASE : BASE + rows] = east_ref[...]
    ext[3, BASE : BASE + rows] = north_ref[...]
    for side, first in ((0, BASE), (1, BASE + rows - 2)):
        for field in range(4):
            stat_send[side, 2 * field : 2 * field + 2] = ext[field, first : first + 2]
    fill(0)
    fill(rows - 8)

    pl.semaphore_wait(barrier, n_slab - 1 + n_mem - 1)

    halo = []
    for side, (d, src, dst) in enumerate(
        ((n_slab - 1, 2, rows + 2), (1, rows, 0))
    ):
        target = (slab_of(d), z)
        halo.append(
            pltpu.make_async_remote_copy(
                src_ref=stat_send.at[side],
                dst_ref=stat_recv.at[side],
                send_sem=halo_send.at[2 * side],
                recv_sem=halo_recv.at[2 * side],
                device_id=target,
                device_id_type=MESH,
            )
        )
        halo.append(
            pltpu.make_async_remote_copy(
                src_ref=padded.at[pl.ds(src, 2)],
                dst_ref=padded.at[pl.ds(dst, 2)],
                send_sem=halo_send.at[2 * side + 1],
                recv_sem=halo_recv.at[2 * side + 1],
                device_id=target,
                device_id_type=MESH,
            )
        )
    for copy in halo:
        copy.start()

    def fill_rest(i, carry):
        fill(pl.multiple_of(8 * i, 8))
        return carry

    lax.fori_loop(1, rows // 8 - 1, fill_rest, 0, unroll=2)

    for copy in staged[5:]:
        copy.wait()
    offsets = offset_ref[...]
    batch_at = lax.broadcasted_iota(jnp.int32, offsets.shape, 0)
    owner_rows = jnp.zeros(offsets.shape, jnp.int32)
    for b in range(batches):
        owner_rows = jnp.where(batch_at == b, owner_ref[b] * rows, owner_rows)
    site_row = (owner_rows + offsets // width).astype(F32)
    site_col = (offsets % width).astype(F32)
    sites[0:batches] = site_row
    sites[batches : 2 * batches] = site_col
    line_of[...] = jnp.where(owner_rows == s * rows, offsets // width, -1)
    for b in range(batches):
        column = (offsets % width)[b : b + 1]
        for first in range(0, width, nobs):
            at = lax.broadcasted_iota(jnp.int32, (nobs, nobs), 0) + first
            column_of[b, first : first + nobs] = (at == column).astype(F32).astype(BF16)
    sea[...] = wet.astype(BF16)
    wet_cols[...] = land_ref[:, pl.ds(pl.multiple_of(z * LANES, LANES), LANES)].astype(F32)

    tall = ext.shape[1]
    lane = lax.broadcasted_iota(jnp.int32, (1, width), 1)
    not_last = (lane < width - 1).astype(F32)
    not_first = (lane > 0).astype(F32)

    def coefficients(first, count):
        conduct, open_, east, north = (ext[f, first : first + count + 2] for f in range(4))

        def leave_enter(near, near_open, far, far_open, flow):
            diffuse = jnp.sqrt(near * far)
            opened = near_open * far_open
            return (
                diffuse + opened * jnp.maximum(flow, 0.0),
                diffuse - opened * jnp.minimum(flow, 0.0),
            )

        mid = slice(1, count + 1)
        c, o = conduct[mid], open_[mid]
        c_next = pltpu.roll(c, width - 1, 1) * not_last
        o_next = pltpu.roll(o, width - 1, 1) * not_last
        out_e, in_e = leave_enter(c, o, c_next, o_next, east[mid])
        out_w = pltpu.roll(out_e, 1, 1) * not_first
        in_w = pltpu.roll(in_e, 1, 1) * not_first
        out_n, in_n = leave_enter(
            conduct[: count + 1], open_[: count + 1], conduct[1:], open_[1:], north[: count + 1]
        )
        where = slice(first + 1, first + 1 + count)
        coef[0, where] = o * (1.0 - out_e - in_w - out_n[1:] - in_n[:-1])
        coef[1, where] = o * in_e
        coef[2, where] = o * out_w
        coef[3, where] = o * in_n[1:]
        coef[4, where] = o * out_n[:-1]


    def stencil(source, at, row):
        def c(i):
            return jnp.broadcast_to(coef[i, pl.ds(row + BASE, 1), :], (OWN, width))

        here = source[at]
        return (
            c(0) * here
            + c(1) * pltpu.roll(here, width - 1, 1)
            + c(2) * pltpu.roll(here, 1, 1)
            + c(3) * source[at + 1]
            + c(4) * source[at - 1]
        )

    def first_step(i, carry):
        middle[i] = stencil(padded, i + 1, i - 1)
        return carry

    def second_step(i, carry):
        r = 2 * i
        pair = [stencil(middle, r + 1 + q, r + q) for q in range(2)]
        for q in range(2):
            forecast[r + q] = pair[q]
        value = jnp.concatenate(pair, 0)
        high = value.astype(BF16)
        rest = value - high.astype(F32)
        middle_part, low = split(rest)
        spot = pl.ds(pl.multiple_of(i * 2 * OWN, 2 * OWN), 2 * OWN)
        parts[0, spot] = high
        parts[1, spot] = middle_part
        parts[2, spot] = low
        return carry

    swaps = {}

    def advance(chunk):
        start = 0 if chunk == 0 else chunk * rb + (0 if chunk == 1 else 2)
        stop = rb if chunk == 0 else (chunk + 1) * rb + 2
        lax.fori_loop(start, stop, first_step, 0, unroll=8)
        lax.fori_loop(chunk * rb // 2, (chunk + 1) * rb // 2, second_step, 0, unroll=4)
        for d in range(1, n_mem):
            t = mem_of(d)
            swaps[chunk, d] = pltpu.make_async_remote_copy(
                src_ref=forecast.at[
                    pl.ds(chunk * rb, rb), :, pl.ds(pl.multiple_of(t * LANES, LANES), LANES)
                ],
                dst_ref=states.at[
                    pl.ds(chunk * rb, rb), pl.ds(pl.multiple_of(z * OWN, OWN), OWN), :
                ],
                send_sem=swap_send.at[chunk * n_mem + d],
                recv_sem=swap_recv.at[chunk * n_mem + d],
                device_id=(s, t),
                device_id_type=MESH,
            )

    order = [*range(1, chunks - 1), 0, chunks - 1]
    steps = [(chunk, d) for chunk in order for d in range(1, n_mem)]
    early = EARLY * (n_mem - 1) // 4
    for first in range(8, rows - 8, 8):
        coefficients(BASE - 1 + first, 8)
    for chunk in order:
        if chunk == 0:
            for copy in halo:
                copy.wait()

            low_ok = (s > 0).astype(F32)
            high_ok = (s < n_slab - 1).astype(F32)
            for field in range(4):
                ext[field, BASE - 2 : BASE] = stat_recv[1, 2 * field : 2 * field + 2] * low_ok
                ext[field, BASE + rows : BASE + rows + 2] = (
                    stat_recv[0, 2 * field : 2 * field + 2] * high_ok
                )
            for first in (0, rows - 8):
                coefficients(BASE - 1 + first, 8)
            coefficients(BASE - 2, 1)
            coefficients(BASE + rows - 1, 1)
        advance(chunk)
        for step in steps[:early]:
            if step[0] == chunk:
                swaps[step].start()
    states[:, pl.ds(pl.multiple_of(z * OWN, OWN), OWN), :] = forecast[
        :, :, pl.ds(pl.multiple_of(z * LANES, LANES), LANES)
    ]

    per_batch = nobs // LANES

    def reduce_to(t):
        return pltpu.make_async_remote_copy(
            src_ref=picked.at[lax.rem(t, n_piece)],
            dst_ref=reduce_buf.at[s],
            send_sem=reduce_send.at[t],
            recv_sem=reduce_recv.at[s],
            device_id=(t, z),
            device_id_type=MESH,
        )

    def reduce_from(t):
        return pltpu.make_async_remote_copy(
            src_ref=picked.at[mine],
            dst_ref=reduce_buf.at[t],
            send_sem=reduce_send.at[t],
            recv_sem=reduce_recv.at[t],
            device_id=(t, z),
            device_id_type=MESH,
        )

    def pick_batch(b, carry):
        line = line_of[pl.ds(b, 1), :]
        chosen_column = column_of[b]
        tracer = jnp.zeros((OWN, nobs), F32)
        at_line = lax.broadcasted_iota(jnp.int32, (rows, OWN, nobs), 0) == line[None]
        for part in range(3):
            part_here = quick(parts[part], chosen_column).reshape(rows, OWN, nobs)
            tracer = tracer + jnp.sum(jnp.where(at_line, part_here, 0.0), axis=0)
        sea_part = quick(sea[...], chosen_column)
        at_row = lax.broadcasted_iota(jnp.int32, (rows, nobs), 0)
        found = jnp.sum(jnp.where(line == at_row, sea_part, 0.0), axis=0, keepdims=True)
        for q in range(per_batch):
            lanes = slice(LANES * q, LANES * (q + 1))
            picked[b * per_batch + q, 0:OWN] = tracer[:, lanes]
            picked[b * per_batch + q, OWN : 2 * OWN] = jnp.broadcast_to(
                found[:, lanes], (OWN, LANES)
            )
            for group in range(0, n_slab, n_piece):
                t = group + b * per_batch + q

                @pl.when(t != s)
                def _():
                    reduce_to(t).start()

        return carry

    lax.fori_loop(0, batches, pick_batch, 0, unroll=2)

    flipped = sites[...].T
    for b in range(batches - 1):
        row_j = flipped[:, b : b + 1]
        col_j = flipped[:, batches + b : batches + b + 1]
        for later in range(b + 1, batches):
            g_row = row_j - sites[later : later + 1]
            g_col = col_j - sites[batches + later : batches + later + 1]
            tapers[b, :, nobs * later : nobs * (later + 1)] = jnp.exp(
                -rate * (g_row * g_row + g_col * g_col)
            )

    total = picked[mine]
    for d in range(1, n_slab):
        reduce_from(slab_of(d)).wait_recv()
        total = total + reduce_buf[slab_of(d)]
    piece[...] = total

    own_rows = pl.ds(pl.multiple_of(z * OWN, OWN), OWN)
    rings = []
    for d in range(1, n_mem):
        rings.append(
            pltpu.make_async_remote_copy(
                src_ref=piece.at[pl.ds(0, OWN)],
                dst_ref=gathered.at[own_rows],
                send_sem=ring_send.at[d],
                recv_sem=ring_recv.at[d],
                device_id=(s, mem_of(d)),
                device_id_type=MESH,
            )
        )
    for copy in rings:
        copy.start()
    gathered[own_rows] = total[0:OWN]
    gathered[members : members + OWN] = total[OWN : 2 * OWN]
    row0 = (s * rows).astype(F32)
    col0 = (z * LANES).astype(F32)
    columns = lax.broadcasted_iota(jnp.int32, (1, LANES), 1).astype(F32) + col0
    for b in range(batches):
        gap = flipped[:, batches + b : batches + b + 1] - columns
        column_taper[b] = jnp.exp(-rate * (gap * gap))
        row_site[b] = jnp.broadcast_to(flipped[:, b : b + 1], (nobs, LANES)) - row0
        base_misfit[b] = value_ref[b : b + 1] + jnp.sqrt(var_ref[b : b + 1]) * noise_ref[b]
    for copy in rings:
        copy.wait_recv()


    own_lanes = pl.ds(pl.multiple_of(mine * LANES, LANES), LANES)
    shares = []
    for d in range(1, n_piece):
        shares.append(
            pltpu.make_async_remote_copy(
                src_ref=gathered,
                dst_ref=site_cols.at[:, own_lanes],
                send_sem=share_send.at[d],
                recv_sem=share_recv.at[mine],
                device_id=(piece_of(d), z),
                device_id_type=MESH,
            )
        )
    for copy in shares:
        copy.start()
    for step in steps[early:]:
        swaps[step].start()
    site_cols[:, own_lanes] = gathered[...]

    def wait_pieces(which):
        for p in which:

            @pl.when(p != mine)
            def _():
                pltpu.make_async_remote_copy(
                    src_ref=gathered,
                    dst_ref=site_cols.at[:, pl.ds(p * LANES, LANES)],
                    send_sem=share_send.at[p],
                    recv_sem=share_recv.at[p],
                    device_id=(piece_of(1), z),
                    device_id_type=MESH,
                ).wait_recv()


    eye = (
        lax.broadcasted_iota(jnp.int32, (members, 2 * members), 0)
        == lax.broadcasted_iota(jnp.int32, (members, 2 * members), 1)
    ).astype(F32)
    wait_pieces(range(per_batch))
    for b in range(batches):
        now = slice(nobs * b, nobs * (b + 1))
        priors = site_cols[0:members, now]
        deviations = priors - jnp.mean(priors, axis=0, keepdims=True)
        inverse_var = 1.0 / var_ref[b : b + 1]
        misfit = base_misfit[b] - priors
        system = contract(
            deviations * inverse_var, jnp.concatenate([deviations, misfit], 0), (1, 1)
        ) + eye * (members - 1.0)
        high, low = split(deviations.T)
        dcat[b] = jnp.concatenate([high, high, low], 1)
        solved = solve_spd(system)
        if b == 0:
            wait_pieces(range(per_batch, n_piece))
        weights = (misfit - contract(solved, deviations, (0, 0))) * (
            inverse_var * (1.0 / (members - 1))
        )
        high, low = split(weights)
        wcat[b] = jnp.concatenate([high, low], 0)
        if b < batches - 1:
            rest = slice(nobs * (b + 1), total_obs)
            values = site_cols[0:members, rest]
            anomalies = values - jnp.mean(values, axis=0, keepdims=True)
            high, low = split(anomalies)
            covariance = quick(dcat[b], jnp.concatenate([high, low, high], 0))
            high, low = split(tapers[b, :, rest] * covariance)
            both = quick(wcat[b], high)
            change = both[:members] + both[members:] + quick(wcat[b, 0:members], low)
            site_cols[0:members, rest] = (
                values + change * site_cols[members : members + 1, rest]
            )

    for chunk in order:
        for d in range(1, n_mem):
            swaps[chunk, d].wait_recv()
        first = chunk * rb
        wet_here = jnp.concatenate(
            [wet_cols[first + q : first + q + 1] * math.exp(-rate * q * q) for q in range(rb)], 1
        )
        here = jnp.concatenate([states[first + q] for q in range(rb)], 1)

        def assimilate(b, here):
            anomalies = here - jnp.mean(here, axis=0, keepdims=True)
            high, low = split(anomalies)
            covariance = quick(dcat[b], jnp.concatenate([high, low, high], 0))
            gap = row_site[b] - float(first)
            step = jnp.exp((2.0 * rate) * gap)
            taper = jnp.exp(-rate * (gap * gap)) * column_taper[b]
            weighted = []
            for q in range(rb):
                weighted.append(covariance[:, LANES * q : LANES * (q + 1)] * taper)
                taper = taper * step
            high, low = split(jnp.concatenate(weighted, 1))
            both = quick(wcat[b], high)
            change = both[:members] + both[members:] + quick(wcat[b, 0:members], low)
            return here + change * wet_here

        here = lax.fori_loop(0, batches, assimilate, here)
        for q in range(rb):
            out_ref[pl.ds(first + q, members, stride=rows), :] = here[
                :, LANES * q : LANES * (q + 1)
            ]

    for d in range(1, n_slab):
        reduce_from(slab_of(d)).wait_send()
    for copy in [*swaps.values(), *rings, *shares]:
        copy.wait_send()


def geometry_of(mesh_shape, rows, batches, nobs):
    n_piece = batches * nobs // LANES
    return mesh_shape["slab"], mesh_shape["mem"], n_piece, rows // 4


def on_device(
    geometry,
    prior_concentrations,
    kappa,
    east_face_transport,
    v_north,
    land,
    obs_owner,
    obs_offset,
    obs_value,
    obs_var,
    obs_noise,
):
    n_slab, n_mem, n_piece, rb = geometry
    own, rows, width = prior_concentrations.shape
    batches, nobs = obs_value.shape
    members = own * n_mem
    chunks = rows // rb
    tall = rows + 2 * BASE
    vmem = pl.BlockSpec(memory_space=pltpu.VMEM)
    smem = pl.BlockSpec(memory_space=pltpu.SMEM)
    hbm = pl.BlockSpec(memory_space=pltpu.HBM)
    dma = pltpu.SemaphoreType.DMA
    out = pl.pallas_call(
        functools.partial(kernel, geometry),
        out_shape=jax.ShapeDtypeStruct((members * rows, LANES), F32),
        in_specs=[hbm] * 5 + [smem] + [hbm] * 4,
        out_specs=vmem,
        scratch_shapes=[
            pltpu.VMEM((own, rows, width), F32),
            pltpu.VMEM((rows, width), F32),
            pltpu.VMEM((rows, width), F32),
            pltpu.VMEM((rows, width), F32),
            pltpu.VMEM((rows, width), jnp.int32),
            pltpu.VMEM((batches, nobs), jnp.int32),
            pltpu.VMEM((batches, nobs), F32),
            pltpu.VMEM((batches, nobs), F32),
            pltpu.VMEM((batches, members, nobs), F32),
            pltpu.VMEM((rows + 4, own, width), F32),
            pltpu.VMEM((rows + 2, own, width), F32),
            pltpu.VMEM((rows, own, width), F32),
            pltpu.VMEM((rows, members, LANES), F32),
            pltpu.VMEM((2, 8, width), F32),
            pltpu.VMEM((2, 8, width), F32),
            pltpu.VMEM((4, tall, width), F32),
            pltpu.VMEM((5, tall, width), F32),
            pltpu.VMEM((3, rows * own, width), BF16),
            pltpu.VMEM((batches, width, nobs), BF16),
            pltpu.VMEM((batches, nobs), jnp.int32),
            pltpu.VMEM((rows, width), BF16),
            pltpu.VMEM((n_piece, 2 * own, LANES), F32),
            pltpu.VMEM((n_slab, 2 * own, LANES), F32),
            pltpu.VMEM((2 * own, LANES), F32),
            pltpu.VMEM((members + own, LANES), F32),
            pltpu.VMEM((2 * batches, nobs), F32),
            pltpu.VMEM((batches - 1, nobs, batches * nobs), F32),
            pltpu.VMEM((batches, members, nobs), F32),
            pltpu.VMEM((batches, nobs, 3 * members), BF16),
            pltpu.VMEM((batches, 2 * members, nobs), BF16),
            pltpu.VMEM((batches, nobs, LANES), F32),
            pltpu.VMEM((batches, nobs, LANES), F32),
            pltpu.VMEM((rows, LANES), F32),
            pltpu.VMEM((members + own, batches * nobs), F32),
            dma((9,)),
            dma((4,)),
            dma((4,)),
            dma((n_slab,)),
            dma((n_slab,)),
            dma((n_mem,)),
            dma((n_mem,)),
            dma((n_piece,)),
            dma((n_piece,)),
            dma((chunks * n_mem,)),
            dma((chunks * n_mem,)),
        ],
        compiler_params=pltpu.CompilerParams(
            collective_id=0, has_side_effects=True, vmem_limit_bytes=60 << 20
        ),
    )(
        prior_concentrations,
        kappa,
        east_face_transport,
        v_north,
        land,
        obs_owner,
        obs_offset,
        obs_value,
        obs_var,
        jnp.swapaxes(obs_noise, 1, 2),
    )
    return out.reshape(members, rows, LANES)


def solution(mesh):
    placed = (
        P("mem", "slab", None),
        P("slab", None),
        P("slab", None),
        P("slab", None),
        P("slab", None),
        P(),
        P(),
        P(),
        P(),
        P(),
    )

    def whole(*arguments):
        prior, value = arguments[0], arguments[7]
        rows = prior.shape[1] // mesh.shape["slab"]
        geometry = geometry_of(mesh.shape, rows, *value.shape)
        return jax.shard_map(
            functools.partial(on_device, geometry),
            mesh=mesh,
            in_specs=placed,
            out_specs=P(None, "slab", "mem"),
            check_vma=False,
        )(*arguments)

    return whole
```
